32 devices in a mesh: gy: 4 (over z), gx: 8 (over y, x, core).
Axes of the slice: x: 2, y: 2, z: 4, core: 2. Of those that a mesh axis runs over, the one named last changes fastest.
Arguments:
- radiance: bfloat16 [256, 256, 4096], P('gy', 'gx'), may hold values from -64 to 64
- kernel: float32 [3, 3, 4096], replicated, may hold values from 0.05 to 0.5
- test_matrix: bfloat16 [4096, 128], replicated, may hold values from -0.09375 to 0.09375
Outputs:
- basis_out: float32 [256, 256, 128], P('gy', 'gx')
- coeffs: float32 [128, 4096], replicated
The draws below stay inside these ranges and needn't reach their ends.
All inputs are finite; a program needn't handle non-finite values.
Results may differ from the reference program's by a relative error of at most 0.00085.
The reference program's roundings to bfloat16 on the way count: a program that leaves them out, or rounds other values in their place, can miss the bound.
Values may be sent and summed in bfloat16 or wider, within the bound.
A program may use at most 192 MiB of HBM per device.

```python
import math
import jax
import jax.numpy as jnp
from jax import lax

C = 4096
K = 128
TH = 64
H = 256
W = 256
PIXELS = 65536
N_GY = 4


def draw_radiance(key, part):
    key_factor, key_pixel, key_noise = jax.random.split(key, 3)
    channel_factor = jax.random.randint(key_factor, (K, C), -2, 3).astype(jnp.float32)
    octave = (jnp.arange(K, dtype=jnp.int32) * 8 // K).astype(jnp.float32)
    strength = jnp.exp2(-octave - 5.0)
    column_place = jnp.arange(W, dtype=jnp.float32) / W

    def one_row(row_index):
        pixel_factor = jax.random.randint(jax.random.fold_in(key_pixel, row_index), (W, K), -2, 3).astype(jnp.float32)
        low_rank = jnp.dot(pixel_factor * strength, channel_factor, precision=lax.Precision.HIGHEST)
        noise_key = jax.random.fold_in(key_noise, row_index)
        row_place = row_index.astype(jnp.float32) / H
        noise = jax.random.truncated_normal(noise_key, -4.0, 4.0, (W, C), jnp.float32)
        brightness = jnp.exp2(1.5 * (row_place + column_place))
        return ((low_rank + noise) * brightness[:, None]).astype(jnp.bfloat16)
    return lax.map(one_row, jnp.arange(H, dtype=jnp.int32))


def centred(stream_key, extent, scale, bound, kind=jnp.bfloat16):
    result = jax.random.normal(stream_key, extent, jnp.float32) * scale
    return jnp.minimum(jnp.maximum(result, -bound), bound).astype(kind)


def setup_inputs(seed: int = 0) -> dict:
    key_of = jax.random.split(jax.random.key(seed), 4)
    radiance = draw_radiance(jax.random.fold_in(key_of[3], 71), 0)
    kernel = jnp.clip(jnp.exp(jax.random.uniform(key_of[1], (3, 3, C), jnp.float32, math.log(0.05), math.log(0.5))), 0.05, 0.5)
    test_matrix = centred(key_of[2], (C, K), C ** -0.5, 0.09375)
    return dict(radiance=radiance, kernel=kernel, test_matrix=test_matrix)


def smooth_block(padded, kernel, row_total, col_total):
    summed = jnp.zeros((row_total, col_total, padded.shape[2]), jnp.float32)
    for row_shift in range(3):
        for col_shift in range(3):
            window = padded[row_shift:row_shift + row_total, col_shift:col_shift + col_total].astype(jnp.float32)
            summed = summed + kernel[row_shift, col_shift] * window
    return summed.astype(jnp.bfloat16)

def factor_basis(values):
    gram_all = jnp.dot(values.T.astype(jnp.float32), values.astype(jnp.float32), precision=lax.Precision.HIGHEST, preferred_element_type=jnp.float32)
    triangle = jnp.linalg.cholesky(gram_all)
    return lax.linalg.triangular_solve(triangle, values, left_side=False, lower=True, transpose_a=True)

def reference(radiance, kernel, test_matrix):
    zero_row = jnp.zeros((1, W, C), radiance.dtype)

    def one_block(block_index):
        row_start = block_index * TH
        upper_rim = lax.dynamic_slice_in_dim(radiance, jnp.maximum(row_start - 1, 0).astype(jnp.int32), 1, 0)
        lower_rim = lax.dynamic_slice_in_dim(radiance, jnp.minimum(row_start + TH, H - 1).astype(jnp.int32), 1, 0)
        upper_rim = jnp.where(block_index > 0, upper_rim, zero_row)
        lower_rim = jnp.where(block_index < N_GY - 1, lower_rim, zero_row)
        middle = lax.dynamic_slice_in_dim(radiance, row_start.astype(jnp.int32), TH, 0)
        stacked = jnp.concatenate([upper_rim, middle, lower_rim], 0)
        padded = jnp.pad(stacked, ((0, 0), (1, 1), (0, 0)))
        return smooth_block(padded, kernel, TH, W)
    blocks = lax.map(one_block, jnp.arange(N_GY, dtype=jnp.int32))
    flattened = blocks.reshape(H * W, C)
    sketch = jnp.dot(flattened.astype(jnp.float32), test_matrix.astype(jnp.float32), preferred_element_type=jnp.float32)
    first_basis = factor_basis(sketch).astype(jnp.bfloat16)
    range_map = jnp.dot(first_basis.T.astype(jnp.float32), flattened.astype(jnp.float32), preferred_element_type=jnp.float32).astype(jnp.bfloat16)
    second = jnp.dot(flattened.astype(jnp.float32), range_map.T.astype(jnp.float32), preferred_element_type=jnp.float32)
    basis_out = factor_basis(second) * math.sqrt(PIXELS)
    basis_half = basis_out.astype(jnp.bfloat16)
    coeffs = jnp.dot(basis_half.T.astype(jnp.float32), flattened.astype(jnp.float32), preferred_element_type=jnp.float32) * (math.sqrt(C) / PIXELS)
    return (basis_out.reshape(H, W, K), coeffs)
```

```python
import functools
import math

import jax
import jax.numpy as jnp
from jax import lax
from jax.experimental import pallas as pl
from jax.experimental.pallas import tpu as pltpu
from jax.sharding import PartitionSpec as P

MESH = pl.DeviceIdType.MESH
LANES = 128
VMEM_LIMIT = 56 * 1024 * 1024


def bit_of(index, bit):
    return (index // 2**bit) % 2


def flipped(index, mask, bits):
    for bit in range(bits):
        if (mask >> bit) & 1:
            index = index + 2**bit * (1 - 2 * bit_of(index, bit))
    return index


def greet(partners):
    barrier = pltpu.get_barrier_semaphore()
    for partner in partners:
        pl.semaphore_signal(barrier, inc=1, device_id=partner, device_id_type=MESH)
    pl.semaphore_wait(barrier, len(partners))


def shifted_pairs(rows, cols, n_gy, n_gx):
    pairs = []
    for y in range(n_gy):
        for x in range(n_gx):
            if 0 <= y + rows < n_gy and 0 <= x + cols < n_gx:
                pairs.append((y * n_gx + x, (y + rows) * n_gx + x + cols))
    return pairs


def smooth_kernel(x_ref, up_ref, down_ref, left_ref, right_ref, k_ref, t_ref, o_ref, s_ref, l_s, r_s):
    height, width, block = x_ref.shape

    @pl.when(pl.program_id(0) == 0)
    def _():
        s_ref[...] = jnp.zeros_like(s_ref)

    for part in range(block // LANES):
        lanes = pl.ds(part * LANES, LANES)
        left = left_ref[:, lanes].astype(jnp.float32)
        right = right_ref[:, lanes].astype(jnp.float32)
        k = [[k_ref[pl.ds(3 * a + b, 1), lanes] for b in range(3)] for a in range(3)]
        l_s[...] = sum(k[a][0] * left[a : a + height] for a in range(3))
        r_s[...] = sum(k[a][2] * right[a : a + height] for a in range(3))
        place = lax.broadcasted_iota(jnp.int32, (width, LANES), 0)

        def row_out(h, above, here, below):
            p = [k[0][b] * above + k[1][b] * here + k[2][b] * below for b in range(3)]
            before = jnp.where(place == 0, l_s[pl.ds(h, 1), :], pltpu.roll(p[0], 1, 0))
            after = jnp.where(place == width - 1, r_s[pl.ds(h, 1), :], pltpu.roll(p[2], width - 1, 0))
            o_ref[h, :, lanes] = (p[1] + before + after).astype(jnp.bfloat16)

        def step(h, carry):
            above, here = carry
            below = x_ref[h + 1, :, lanes].astype(jnp.float32)
            row_out(h, above, here, below)
            return here, below

        first = (up_ref[:, lanes].astype(jnp.float32), x_ref[0, :, lanes].astype(jnp.float32))
        above, here = lax.fori_loop(0, height - 1, step, first, unroll=3)
        row_out(height - 1, above, here, down_ref[:, lanes].astype(jnp.float32))

    s_ref[...] += jnp.dot(
        o_ref[...].reshape(height * width, block), t_ref[...], preferred_element_type=jnp.float32
    )


def smooth_and_sketch(radiance, kernel, test_matrix):
    height, width, channels = radiance.shape
    k_width = test_matrix.shape[1]
    n_gy, n_gx = lax.axis_size("gy"), lax.axis_size("gx")
    block = 512

    def moved(value, rows, cols):
        return lax.ppermute(value, ("gy", "gx"), shifted_pairs(rows, cols, n_gy, n_gx))

    up = moved(radiance[height - 1], 1, 0)
    down = moved(radiance[0], -1, 0)
    sides = []
    for cols, place in ((1, width - 1), (-1, 0)):
        middle = moved(radiance[:, place], 0, cols)
        top = moved(radiance[height - 1 :, place], 1, cols)
        bottom = moved(radiance[:1, place], -1, cols)
        sides.append(jnp.concatenate([top, middle, bottom], axis=0))
    pixels = height * width
    return pl.pallas_call(
        smooth_kernel,
        grid=(channels // block,),
        in_specs=[
            pl.BlockSpec((height, width, block), lambda i: (0, 0, i)),
            pl.BlockSpec((width, block), lambda i: (0, i)),
            pl.BlockSpec((width, block), lambda i: (0, i)),
            pl.BlockSpec((height + 2, block), lambda i: (0, i)),
            pl.BlockSpec((height + 2, block), lambda i: (0, i)),
            pl.BlockSpec((9, block), lambda i: (0, i)),
            pl.BlockSpec((block, k_width), lambda i: (i, 0)),
        ],
        out_specs=[
            pl.BlockSpec((height, width, block), lambda i: (0, 0, i)),
            pl.BlockSpec((pixels, k_width), lambda i: (0, 0)),
        ],
        out_shape=[
            jax.ShapeDtypeStruct((height, width, channels), jnp.bfloat16),
            jax.ShapeDtypeStruct((pixels, k_width), jnp.float32),
        ],
        scratch_shapes=[
            pltpu.VMEM((height, LANES), jnp.float32),
            pltpu.VMEM((height, LANES), jnp.float32),
        ],
        compiler_params=pltpu.CompilerParams(vmem_limit_bytes=VMEM_LIMIT),
        cost_estimate=pl.CostEstimate(
            flops=pixels * channels * (2 * k_width + 18),
            bytes_accessed=4 * pixels * channels,
            transcendentals=0,
        ),
        name="smooth_sketch",
    )(radiance, up, down, sides[0], sides[1], kernel.reshape(9, channels), test_matrix)


def tree_sum(values):
    while len(values) > 1:
        values = [values[i] + values[i + 1] for i in range(0, len(values), 2)]
    return values[0]


def gram_kernel(n_gy, n_gx, x_ref, o_ref, recv_x, recv_y, mine, sx, rx, sy, ry, sg, rg):
    bits_x, bits_y = n_gx.bit_length() - 1, n_gy.bit_length() - 1
    me_x, me_y = lax.axis_index("gx"), lax.axis_index("gy")
    rows = x_ref.shape[0] // n_gx
    along_x = [flipped(me_x, d, bits_x) for d in range(n_gx)]
    along_y = [flipped(me_y, d, bits_y) for d in range(n_gy)]
    greet([(me_y, p) for p in along_x[1:]] + [(p, me_x) for p in along_y[1:]])

    def block(ref, index):
        return ref.at[pl.ds(pl.multiple_of(index * rows, rows), rows), :]

    copies = []
    for d in range(1, n_gx):
        copy = pltpu.make_async_remote_copy(
            block(x_ref, along_x[d]), recv_x.at[d], sx.at[d], rx.at[d], (me_y, along_x[d]), MESH
        )
        copy.start()
        copies.append(copy)
    for copy in copies:
        copy.wait_recv()
    own = x_ref[pl.ds(pl.multiple_of(me_x * rows, rows), rows), :]
    mine[...] = tree_sum([own] + [recv_x[d] for d in range(1, n_gx)])
    later = []
    for d in range(1, n_gy):
        copy = pltpu.make_async_remote_copy(
            mine, recv_y.at[d], sy.at[d], ry.at[d], (along_y[d], me_x), MESH
        )
        copy.start()
        later.append(copy)
    for copy in later:
        copy.wait_recv()
    total = tree_sum([mine[...]] + [recv_y[d] for d in range(1, n_gy)])
    o_ref[pl.ds(pl.multiple_of(me_x * rows, rows), rows), :] = total
    last = []
    for d in range(1, n_gx):
        copy = pltpu.make_async_remote_copy(
            block(o_ref, me_x), block(o_ref, me_x), sg.at[d], rg.at[d], (me_y, along_x[d]), MESH
        )
        copy.start()
        last.append(copy)
    for d in range(1, n_gx):
        pltpu.make_async_remote_copy(
            block(o_ref, along_x[d]), block(o_ref, along_x[d]), sg.at[d], rg.at[d], (me_y, along_x[d]), MESH
        ).wait_recv()
    for copy in copies + later + last:
        copy.wait_send()


def summed_gram(gram, collective_id):
    n_gy, n_gx = lax.axis_size("gy"), lax.axis_size("gx")
    k = gram.shape[0]
    rows = k // n_gx
    dma = pltpu.SemaphoreType.DMA
    return pl.pallas_call(
        functools.partial(gram_kernel, n_gy, n_gx),
        out_shape=jax.ShapeDtypeStruct(gram.shape, jnp.float32),
        in_specs=[pl.BlockSpec(memory_space=pltpu.VMEM)],
        out_specs=pl.BlockSpec(memory_space=pltpu.VMEM),
        scratch_shapes=[
            pltpu.VMEM((n_gx, rows, k), jnp.float32),
            pltpu.VMEM((n_gy, rows, k), jnp.float32),
            pltpu.VMEM((rows, k), jnp.float32),
            dma((n_gx,)),
            dma((n_gx,)),
            dma((n_gy,)),
            dma((n_gy,)),
            dma((n_gx,)),
            dma((n_gx,)),
        ],
        compiler_params=pltpu.CompilerParams(collective_id=collective_id, has_side_effects=True),
        name="gram_sum",
    )(gram)


def wide_orders(n_gy, n_gx):
    x_bits = [("gx", b) for b in range(n_gx.bit_length() - 1)]
    y_bits = [("gy", b) for b in range(n_gy.bit_length() - 1)]
    first, across = x_bits[:1], x_bits[1:]
    return [first + across + y_bits, first + across[::-1] + y_bits]


def halvings(rows, cols, count):
    shapes = []
    for _ in range(count):
        if rows > 16:
            rows //= 2
        else:
            cols //= 2
        shapes.append((rows, cols))
    return shapes


def wide_kernel(orders, x_ref, o_ref, *scratch):
    steps, chunks = len(orders[0]), len(orders)
    rows, cols = x_ref.shape
    wide = cols // chunks
    work = scratch[0]
    recv = [scratch[1 + q * steps : 1 + (q + 1) * steps] for q in range(chunks)]
    s_send, s_recv, g_send, g_recv = scratch[1 + chunks * steps :]
    me = {"gx": lax.axis_index("gx"), "gy": lax.axis_index("gy")}

    def partner(axis, bit):
        other = dict(me)
        other[axis] = flipped(me[axis], 1 << bit, bit + 1)
        return (other["gy"], other["gx"])

    greet([partner(*which) for which in orders[0]])
    shapes = halvings(rows, wide, steps)
    kept, sent = [], []
    for q in range(chunks):
        row, col = 0, q * wide
        size = (rows, wide)
        kept_q, sent_q = [], []
        for s, (axis, bit) in enumerate(orders[q]):
            mine = bit_of(me[axis], bit)
            h, w = shapes[s]
            if h < size[0]:
                kept_q.append((row + mine * h, col))
                sent_q.append((row + (1 - mine) * h, col))
            else:
                kept_q.append((row, col + mine * w))
                sent_q.append((row, col + (1 - mine) * w))
            row, col = kept_q[-1]
            size = (h, w)
        kept.append(kept_q)
        sent.append(sent_q)

    def region(place, shape):
        row = place[0] if isinstance(place[0], int) else pl.multiple_of(place[0], 16)
        col = place[1] if isinstance(place[1], int) else pl.multiple_of(place[1], LANES)
        return (pl.ds(row, shape[0]), pl.ds(col, shape[1]))

    def reduce_copy(q, s):
        source = x_ref if s == 0 else work
        return pltpu.make_async_remote_copy(
            source.at[region(sent[q][s], shapes[s])],
            recv[q][s],
            s_send.at[q * steps + s],
            s_recv.at[q * steps + s],
            partner(*orders[q][s]),
            MESH,
        )

    def gather_copy(q, s, outgoing):
        place = region(kept[q][s] if outgoing else sent[q][s], shapes[s])
        return pltpu.make_async_remote_copy(
            o_ref.at[place],
            o_ref.at[place],
            g_send.at[q * steps + s],
            g_recv.at[q * steps + s],
            partner(*orders[q][s]),
            MESH,
        )

    for q in range(chunks):
        reduce_copy(q, 0).start()
    for s in range(steps):
        for q in range(chunks):
            reduce_copy(q, s).wait_recv()
            here = region(kept[q][s], shapes[s])
            source = x_ref if s == 0 else work
            total = source[here] + recv[q][s][...]
            if s + 1 < steps:
                work[here] = total
                reduce_copy(q, s + 1).start()
            else:
                o_ref[here] = total.astype(o_ref.dtype)
                gather_copy(q, s, True).start()
    for s in reversed(range(steps)):
        for q in range(chunks):
            gather_copy(q, s, False).wait_recv()
            if s > 0:
                gather_copy(q, s - 1, True).start()
    for s in range(steps):
        for q in range(chunks):
            reduce_copy(q, s).wait_send()
            gather_copy(q, s, True).wait_send()


def summed_wide(values, dtype, collective_id):
    n_gy, n_gx = lax.axis_size("gy"), lax.axis_size("gx")
    orders = wide_orders(n_gy, n_gx)
    rows, cols = values.shape
    steps, chunks = len(orders[0]), len(orders)
    shapes = halvings(rows, cols // chunks, steps)
    dma = pltpu.SemaphoreType.DMA((chunks * steps,))
    return pl.pallas_call(
        functools.partial(wide_kernel, orders),
        out_shape=jax.ShapeDtypeStruct(values.shape, dtype),
        in_specs=[pl.BlockSpec(memory_space=pltpu.VMEM)],
        out_specs=pl.BlockSpec(memory_space=pltpu.VMEM),
        scratch_shapes=[pltpu.VMEM((rows, cols), jnp.float32)]
        + [pltpu.VMEM(shape, jnp.float32) for _ in range(chunks) for shape in shapes]
        + [dma] * 4,
        compiler_params=pltpu.CompilerParams(
            collective_id=collective_id, has_side_effects=True, vmem_limit_bytes=VMEM_LIMIT
        ),
        name="wide_sum",
    )(values)


def factor_basis(values, collective_id):
    local_gram = jnp.dot(
        values.T, values, precision=lax.Precision.HIGHEST, preferred_element_type=jnp.float32
    )
    triangle = jnp.linalg.cholesky(summed_gram(local_gram, collective_id))
    return lax.linalg.triangular_solve(
        triangle, values, left_side=False, lower=True, transpose_a=True
    )


def on_device(radiance, kernel, test_matrix):
    height, breadth, channels = radiance.shape
    devices = lax.axis_size("gy") * lax.axis_size("gx")
    pixel_count = height * breadth * devices
    smoothed, sketch = smooth_and_sketch(radiance, kernel, test_matrix)
    flattened = smoothed.reshape(height * breadth, channels)
    first_basis = factor_basis(sketch, 0).astype(jnp.bfloat16)
    range_map = summed_wide(
        jnp.dot(first_basis.T, flattened, preferred_element_type=jnp.float32), jnp.bfloat16, 2
    )
    second = jnp.dot(flattened, range_map.T, preferred_element_type=jnp.float32)
    basis_out = factor_basis(second, 1) * math.sqrt(pixel_count)
    basis_half = basis_out.astype(jnp.bfloat16)
    projected = jnp.dot(basis_half.T, flattened, preferred_element_type=jnp.float32)
    coeffs = summed_wide(projected, jnp.float32, 3) * (math.sqrt(channels) / pixel_count)
    return (basis_out.reshape(height, breadth, basis_out.shape[1]), coeffs)


def solution(mesh):
    placed = (P("gy", "gx", None), P(), P())
    return jax.shard_map(
        on_device, mesh=mesh, in_specs=placed, out_specs=(P("gy", "gx", None), P()), check_vma=False
    )
```

```python
import functools
import math

import jax
import jax.numpy as jnp
from jax import lax
from jax.experimental import pallas as pl
from jax.experimental.pallas import tpu as pltpu
from jax.sharding import PartitionSpec as P

MESH = pl.DeviceIdType.MESH
LANES = 128
VMEM_LIMIT = 56 * 1024 * 1024


def bit_of(index, bit):
    return (index // 2**bit) % 2


def flipped(index, mask, bits):
    for bit in range(bits):
        if (mask >> bit) & 1:
            index = index + 2**bit * (1 - 2 * bit_of(index, bit))
    return index


def greet(partners):
    barrier = pltpu.get_barrier_semaphore()
    for partner in partners:
        pl.semaphore_signal(barrier, inc=1, device_id=partner, device_id_type=MESH)
    pl.semaphore_wait(barrier, len(partners))


DIRECTIONS = ((1, 0), (-1, 0), (0, 1), (0, -1), (1, 1), (1, -1), (-1, 1), (-1, -1))


def halo_kernel(n_gy, n_gx, x_ref, first_ref, last_ref, corner_ref, *rest):
    outs, (send, recv) = rest[:8], rest[8:]
    height = x_ref.shape[0]
    y, x = lax.axis_index("gy"), lax.axis_index("gx")
    sources = [x_ref.at[height - 1], x_ref.at[0], last_ref, first_ref] + [
        corner_ref.at[i] for i in range(4)
    ]
    barrier = pltpu.get_barrier_semaphore()

    def inside(rows, cols):
        return (y + rows >= 0) & (y + rows < n_gy) & (x + cols >= 0) & (x + cols < n_gx)

    present = 0
    for rows, cols in DIRECTIONS:
        there = inside(rows, cols)
        present = present + jnp.where(there, 1, 0)

        @pl.when(there)
        def _():
            pl.semaphore_signal(
                barrier, inc=1, device_id=(y + rows, x + cols), device_id_type=MESH
            )

    pl.semaphore_wait(barrier, present)

    def copy(i):
        rows, cols = DIRECTIONS[i]
        return pltpu.make_async_remote_copy(
            sources[i], outs[i], send.at[i], recv.at[i], (y + rows, x + cols), MESH
        )

    for i, (rows, cols) in enumerate(DIRECTIONS):

        @pl.when(inside(rows, cols))
        def _():
            copy(i).start()

    for i, (rows, cols) in enumerate(DIRECTIONS):
        arrives = inside(-rows, -cols)

        @pl.when(arrives)
        def _():
            copy(i).wait_recv()

        @pl.when(jnp.logical_not(arrives))
        def _():
            outs[i][...] = jnp.zeros_like(outs[i])

    for i, (rows, cols) in enumerate(DIRECTIONS):

        @pl.when(inside(rows, cols))
        def _():
            copy(i).wait_send()


def halos(radiance, collective_id):
    height, width, channels = radiance.shape
    n_gy, n_gx = lax.axis_size("gy"), lax.axis_size("gx")
    first, last = radiance[:, 0], radiance[:, width - 1]
    corners = jnp.stack([last[height - 1], first[height - 1], last[0], first[0]])
    corners = corners.reshape(4, 16, channels // 16)
    shapes = [(width, channels)] * 2 + [(height, channels)] * 2 + [(16, channels // 16)] * 4
    vmem = pl.BlockSpec(memory_space=pltpu.VMEM)
    outs = pl.pallas_call(
        functools.partial(halo_kernel, n_gy, n_gx),
        out_shape=[jax.ShapeDtypeStruct(shape, radiance.dtype) for shape in shapes],
        in_specs=[pl.BlockSpec(memory_space=pl.ANY), vmem, vmem, vmem],
        out_specs=[vmem] * 8,
        scratch_shapes=[pltpu.SemaphoreType.DMA((8,)), pltpu.SemaphoreType.DMA((8,))],
        compiler_params=pltpu.CompilerParams(collective_id=collective_id, has_side_effects=True),
        name="halo",
    )(radiance, first, last, corners)
    return outs[:4], jnp.stack(outs[4:]).reshape(4, channels)


def smooth_kernel(
    x_ref, up_ref, down_ref, left_ref, right_ref, c_ref, k_ref, t_ref, o_ref, s_ref, side, l_s, r_s
):
    height, width, block = x_ref.shape

    @pl.when(pl.program_id(0) == 0)
    def _():
        s_ref[...] = jnp.zeros_like(s_ref)

    for part in range(block // LANES):
        lanes = pl.ds(part * LANES, LANES)
        k = [[k_ref[pl.ds(3 * a + b, 1), lanes] for b in range(3)] for a in range(3)]
        corners = c_ref[:, lanes].astype(jnp.float32)
        for b, middle, corner, sums in ((0, left_ref, 0, l_s), (2, right_ref, 1, r_s)):
            side[pl.ds(8, height), :] = middle[:, lanes].astype(jnp.float32)
            side[pl.ds(7, 1), :] = corners[corner : corner + 1]
            side[pl.ds(8 + height, 1), :] = corners[corner + 2 : corner + 3]
            sums[...] = sum(k[a][b] * side[pl.ds(7 + a, height), :] for a in range(3))
        place = lax.broadcasted_iota(jnp.int32, (width, LANES), 0)

        def row_out(h, above, here, below):
            p = [k[0][b] * above + k[1][b] * here + k[2][b] * below for b in range(3)]
            before = jnp.where(place == 0, l_s[pl.ds(h, 1), :], pltpu.roll(p[0], 1, 0))
            after = jnp.where(place == width - 1, r_s[pl.ds(h, 1), :], pltpu.roll(p[2], width - 1, 0))
            o_ref[h, :, lanes] = (p[1] + before + after).astype(jnp.bfloat16)

        def step(h, carry):
            above, here = carry
            below = x_ref[h + 1, :, lanes].astype(jnp.float32)
            row_out(h, above, here, below)
            return here, below

        first = (up_ref[:, lanes].astype(jnp.float32), x_ref[0, :, lanes].astype(jnp.float32))
        above, here = lax.fori_loop(0, height - 1, step, first, unroll=3)
        row_out(height - 1, above, here, down_ref[:, lanes].astype(jnp.float32))

    s_ref[...] += jnp.dot(
        o_ref[...].reshape(height * width, block), t_ref[...], preferred_element_type=jnp.float32
    )


def smooth_and_sketch(radiance, kernel, test_matrix):
    height, width, channels = radiance.shape
    k_width = test_matrix.shape[1]
    block = 512
    (up, down, left, right), corners = halos(radiance, 4)
    pixels = height * width
    return pl.pallas_call(
        smooth_kernel,
        grid=(channels // block,),
        in_specs=[
            pl.BlockSpec((height, width, block), lambda i: (0, 0, i)),
            pl.BlockSpec((width, block), lambda i: (0, i)),
            pl.BlockSpec((width, block), lambda i: (0, i)),
            pl.BlockSpec((height, block), lambda i: (0, i)),
            pl.BlockSpec((height, block), lambda i: (0, i)),
            pl.BlockSpec((4, block), lambda i: (0, i)),
            pl.BlockSpec((9, block), lambda i: (0, i)),
            pl.BlockSpec((block, k_width), lambda i: (i, 0)),
        ],
        out_specs=[
            pl.BlockSpec((height, width, block), lambda i: (0, 0, i)),
            pl.BlockSpec((pixels, k_width), lambda i: (0, 0)),
        ],
        out_shape=[
            jax.ShapeDtypeStruct((height, width, channels), jnp.bfloat16),
            jax.ShapeDtypeStruct((pixels, k_width), jnp.float32),
        ],
        scratch_shapes=[
            pltpu.VMEM((height + 16, LANES), jnp.float32),
            pltpu.VMEM((height, LANES), jnp.float32),
            pltpu.VMEM((height, LANES), jnp.float32),
        ],
        compiler_params=pltpu.CompilerParams(vmem_limit_bytes=VMEM_LIMIT),
        cost_estimate=pl.CostEstimate(
            flops=pixels * channels * (2 * k_width + 18),
            bytes_accessed=4 * pixels * channels,
            transcendentals=0,
        ),
        name="smooth_sketch",
    )(radiance, up, down, left, right, corners, kernel.reshape(9, channels), test_matrix)


def tree_sum(values):
    while len(values) > 1:
        values = [values[i] + values[i + 1] for i in range(0, len(values), 2)]
    return values[0]


def gram_kernel(n_gy, n_gx, x_ref, o_ref, recv_x, recv_y, mine, sx, rx, sy, ry, sg, rg):
    bits_x, bits_y = n_gx.bit_length() - 1, n_gy.bit_length() - 1
    me_x, me_y = lax.axis_index("gx"), lax.axis_index("gy")
    rows = x_ref.shape[0] // n_gx
    along_x = [flipped(me_x, d, bits_x) for d in range(n_gx)]
    along_y = [flipped(me_y, d, bits_y) for d in range(n_gy)]
    greet([(me_y, p) for p in along_x[1:]] + [(p, me_x) for p in along_y[1:]])

    def block(ref, index):
        return ref.at[pl.ds(pl.multiple_of(index * rows, rows), rows), :]

    copies = []
    for d in range(1, n_gx):
        copy = pltpu.make_async_remote_copy(
            block(x_ref, along_x[d]), recv_x.at[d], sx.at[d], rx.at[d], (me_y, along_x[d]), MESH
        )
        copy.start()
        copies.append(copy)
    for copy in copies:
        copy.wait_recv()
    own = x_ref[pl.ds(pl.multiple_of(me_x * rows, rows), rows), :]
    mine[...] = tree_sum([own] + [recv_x[d] for d in range(1, n_gx)])
    later = []
    for d in range(1, n_gy):
        copy = pltpu.make_async_remote_copy(
            mine, recv_y.at[d], sy.at[d], ry.at[d], (along_y[d], me_x), MESH
        )
        copy.start()
        later.append(copy)
    for copy in later:
        copy.wait_recv()
    total = tree_sum([mine[...]] + [recv_y[d] for d in range(1, n_gy)])
    o_ref[pl.ds(pl.multiple_of(me_x * rows, rows), rows), :] = total
    last = []
    for d in range(1, n_gx):
        copy = pltpu.make_async_remote_copy(
            block(o_ref, me_x), block(o_ref, me_x), sg.at[d], rg.at[d], (me_y, along_x[d]), MESH
        )
        copy.start()
        last.append(copy)
    for d in range(1, n_gx):
        pltpu.make_async_remote_copy(
            block(o_ref, along_x[d]), block(o_ref, along_x[d]), sg.at[d], rg.at[d], (me_y, along_x[d]), MESH
        ).wait_recv()
    for copy in copies + later + last:
        copy.wait_send()


def summed_gram(gram, collective_id):
    n_gy, n_gx = lax.axis_size("gy"), lax.axis_size("gx")
    k = gram.shape[0]
    rows = k // n_gx
    dma = pltpu.SemaphoreType.DMA
    return pl.pallas_call(
        functools.partial(gram_kernel, n_gy, n_gx),
        out_shape=jax.ShapeDtypeStruct(gram.shape, jnp.float32),
        in_specs=[pl.BlockSpec(memory_space=pltpu.VMEM)],
        out_specs=pl.BlockSpec(memory_space=pltpu.VMEM),
        scratch_shapes=[
            pltpu.VMEM((n_gx, rows, k), jnp.float32),
            pltpu.VMEM((n_gy, rows, k), jnp.float32),
            pltpu.VMEM((rows, k), jnp.float32),
            dma((n_gx,)),
            dma((n_gx,)),
            dma((n_gy,)),
            dma((n_gy,)),
            dma((n_gx,)),
            dma((n_gx,)),
        ],
        compiler_params=pltpu.CompilerParams(collective_id=collective_id, has_side_effects=True),
        name="gram_sum",
    )(gram)


def wide_orders(n_gy, n_gx):
    x_bits = [("gx", b) for b in range(n_gx.bit_length() - 1)]
    y_bits = [("gy", b) for b in range(n_gy.bit_length() - 1)]
    first, across = x_bits[:1], x_bits[1:]
    return [first + across + y_bits, first + across[::-1] + y_bits]


def halvings(rows, cols, count):
    shapes = []
    for _ in range(count):
        if rows > 16:
            rows //= 2
        else:
            cols //= 2
        shapes.append((rows, cols))
    return shapes


def wide_kernel(orders, x_ref, o_ref, *scratch):
    steps, chunks = len(orders[0]), len(orders)
    rows, cols = x_ref.shape
    wide = cols // chunks
    work = scratch[0]
    recv = [scratch[1 + q * steps : 1 + (q + 1) * steps] for q in range(chunks)]
    s_send, s_recv, g_send, g_recv = scratch[1 + chunks * steps :]
    me = {"gx": lax.axis_index("gx"), "gy": lax.axis_index("gy")}

    def partner(axis, bit):
        other = dict(me)
        other[axis] = flipped(me[axis], 1 << bit, bit + 1)
        return (other["gy"], other["gx"])

    greet([partner(*which) for which in orders[0]])
    shapes = halvings(rows, wide, steps)
    kept, sent = [], []
    for q in range(chunks):
        row, col = 0, q * wide
        size = (rows, wide)
        kept_q, sent_q = [], []
        for s, (axis, bit) in enumerate(orders[q]):
            mine = bit_of(me[axis], bit)
            h, w = shapes[s]
            if h < size[0]:
                kept_q.append((row + mine * h, col))
                sent_q.append((row + (1 - mine) * h, col))
            else:
                kept_q.append((row, col + mine * w))
                sent_q.append((row, col + (1 - mine) * w))
            row, col = kept_q[-1]
            size = (h, w)
        kept.append(kept_q)
        sent.append(sent_q)

    def region(place, shape):
        row = place[0] if isinstance(place[0], int) else pl.multiple_of(place[0], 16)
        col = place[1] if isinstance(place[1], int) else pl.multiple_of(place[1], LANES)
        return (pl.ds(row, shape[0]), pl.ds(col, shape[1]))

    def reduce_copy(q, s):
        source = x_ref if s == 0 else work
        return pltpu.make_async_remote_copy(
            source.at[region(sent[q][s], shapes[s])],
            recv[q][s],
            s_send.at[q * steps + s],
            s_recv.at[q * steps + s],
            partner(*orders[q][s]),
            MESH,
        )

    def gather_copy(q, s, outgoing):
        place = region(kept[q][s] if outgoing else sent[q][s], shapes[s])
        return pltpu.make_async_remote_copy(
            o_ref.at[place],
            o_ref.at[place],
            g_send.at[q * steps + s],
            g_recv.at[q * steps + s],
            partner(*orders[q][s]),
            MESH,
        )

    for q in range(chunks):
        reduce_copy(q, 0).start()
    for s in range(steps):
        for q in range(chunks):
            reduce_copy(q, s).wait_recv()
            here = region(kept[q][s], shapes[s])
            source = x_ref if s == 0 else work
            total = source[here] + recv[q][s][...]
            if s + 1 < steps:
                work[here] = total
                reduce_copy(q, s + 1).start()
            else:
                o_ref[here] = total.astype(o_ref.dtype)
                gather_copy(q, s, True).start()
    for s in reversed(range(steps)):
        for q in range(chunks):
            gather_copy(q, s, False).wait_recv()
            if s > 0:
                gather_copy(q, s - 1, True).start()
    for s in range(steps):
        for q in range(chunks):
            reduce_copy(q, s).wait_send()
            gather_copy(q, s, True).wait_send()


def summed_wide(values, dtype, collective_id):
    n_gy, n_gx = lax.axis_size("gy"), lax.axis_size("gx")
    orders = wide_orders(n_gy, n_gx)
    rows, cols = values.shape
    steps, chunks = len(orders[0]), len(orders)
    shapes = halvings(rows, cols // chunks, steps)
    dma = pltpu.SemaphoreType.DMA((chunks * steps,))
    return pl.pallas_call(
        functools.partial(wide_kernel, orders),
        out_shape=jax.ShapeDtypeStruct(values.shape, dtype),
        in_specs=[pl.BlockSpec(memory_space=pltpu.VMEM)],
        out_specs=pl.BlockSpec(memory_space=pltpu.VMEM),
        scratch_shapes=[pltpu.VMEM((rows, cols), jnp.float32)]
        + [pltpu.VMEM(shape, jnp.float32) for _ in range(chunks) for shape in shapes]
        + [dma] * 4,
        compiler_params=pltpu.CompilerParams(
            collective_id=collective_id, has_side_effects=True, vmem_limit_bytes=VMEM_LIMIT
        ),
        name="wide_sum",
    )(values)


def inverse_factor_kernel(gram_ref, o_ref, state):
    size = gram_ref.shape[0]
    row = lax.broadcasted_iota(jnp.int32, (size, size), 0)
    col = lax.broadcasted_iota(jnp.int32, (size, size), 1)
    state[:, :size] = gram_ref[...]
    state[:, size:] = jnp.where(row == col, 1.0, 0.0)
    shape = (8, size)
    place = lax.broadcasted_iota(jnp.int32, shape, 0)
    for start in range(0, size, 8):
        left = state[start : start + 8, :size]
        right = state[start : start + 8, size:]
        columns = [
            jnp.broadcast_to(left[:, start + j : start + j + 1], shape) for j in range(8)
        ]
        scale = jnp.zeros(shape, jnp.float32)
        for j in range(8):

            def pivot_row(value):
                return jnp.broadcast_to(value[j : j + 1], shape)

            inverse = 1.0 / pivot_row(columns[j])
            scale = jnp.where(place == j, inverse, scale)
            if j == 7:
                break
            factor = jnp.where(place > j, columns[j] * inverse, 0.0)
            left = left - factor * pivot_row(left)
            right = right - factor * pivot_row(right)
            for i in range(j + 1, 8):
                columns[i] = columns[i] - factor * pivot_row(columns[i])
        o_ref[start : start + 8, :] = right * jnp.sqrt(scale)
        if start + 8 < size:
            update = jnp.dot(
                (left * scale).T,
                jnp.concatenate([left, right], axis=1),
                precision=lax.Precision.HIGHEST,
                preferred_element_type=jnp.float32,
            )
            state[start + 8 :, :] = state[start + 8 :, :] - update[start + 8 :, :]


def inverse_factor(gram):
    size = gram.shape[0]
    return pl.pallas_call(
        inverse_factor_kernel,
        out_shape=jax.ShapeDtypeStruct(gram.shape, jnp.float32),
        in_specs=[pl.BlockSpec(memory_space=pltpu.VMEM)],
        out_specs=pl.BlockSpec(memory_space=pltpu.VMEM),
        scratch_shapes=[pltpu.VMEM((size, 2 * size), jnp.float32)],
        name="inverse_factor",
    )(gram)


def factor_basis(values, collective_id):
    local_gram = jnp.dot(
        values.T, values, precision=lax.Precision.HIGHEST, preferred_element_type=jnp.float32
    )
    inverse = inverse_factor(summed_gram(local_gram, collective_id))
    return jnp.dot(
        values, inverse.T, precision=lax.Precision.HIGHEST, preferred_element_type=jnp.float32
    )


def on_device(radiance, kernel, test_matrix):
    height, breadth, channels = radiance.shape
    devices = lax.axis_size("gy") * lax.axis_size("gx")
    pixel_count = height * breadth * devices
    smoothed, sketch = smooth_and_sketch(radiance, kernel, test_matrix)
    flattened = smoothed.reshape(height * breadth, channels)
    first_basis = factor_basis(sketch, 0).astype(jnp.bfloat16)
    range_map = summed_wide(
        jnp.dot(first_basis.T, flattened, preferred_element_type=jnp.float32), jnp.bfloat16, 2
    )
    second = jnp.dot(flattened, range_map.T, preferred_element_type=jnp.float32)
    basis_out = factor_basis(second, 1) * math.sqrt(pixel_count)
    basis_half = basis_out.astype(jnp.bfloat16)
    projected = jnp.dot(basis_half.T, flattened, preferred_element_type=jnp.float32)
    coeffs = summed_wide(projected, jnp.float32, 3) * (math.sqrt(channels) / pixel_count)
    return (basis_out.reshape(height, breadth, basis_out.shape[1]), coeffs)


def solution(mesh):
    placed = (P("gy", "gx", None), P(), P())
    return jax.shard_map(
        on_device, mesh=mesh, in_specs=placed, out_specs=(P("gy", "gx", None), P()), check_vma=False
    )
```

```python
import functools
import math

import jax
import jax.numpy as jnp
from jax import lax
from jax.experimental import pallas as pl
from jax.experimental.pallas import tpu as pltpu
from jax.sharding import PartitionSpec as P

MESH = pl.DeviceIdType.MESH
LANES = 128
VMEM_LIMIT = 56 * 1024 * 1024


def bit_of(index, bit):
    return (index // 2**bit) % 2


def flipped(index, mask, bits):
    for bit in range(bits):
        if (mask >> bit) & 1:
            index = index + 2**bit * (1 - 2 * bit_of(index, bit))
    return index


def greet(partners):
    barrier = pltpu.get_barrier_semaphore()
    for partner in partners:
        pl.semaphore_signal(barrier, inc=1, device_id=partner, device_id_type=MESH)
    pl.semaphore_wait(barrier, len(partners))


DIRECTIONS = ((1, 0), (-1, 0), (0, 1), (0, -1), (1, 1), (1, -1), (-1, 1), (-1, -1))


def halo_kernel(n_gy, n_gx, x_ref, first_ref, last_ref, corner_ref, *rest):
    outs, (send, recv) = rest[:8], rest[8:]
    height = x_ref.shape[0]
    y, x = lax.axis_index("gy"), lax.axis_index("gx")
    sources = [x_ref.at[height - 1], x_ref.at[0], last_ref, first_ref] + [
        corner_ref.at[i] for i in range(4)
    ]
    barrier = pltpu.get_barrier_semaphore()

    def inside(rows, cols):
        return (y + rows >= 0) & (y + rows < n_gy) & (x + cols >= 0) & (x + cols < n_gx)

    present = 0
    for rows, cols in DIRECTIONS:
        there = inside(rows, cols)
        present = present + jnp.where(there, 1, 0)

        @pl.when(there)
        def _():
            pl.semaphore_signal(
                barrier, inc=1, device_id=(y + rows, x + cols), device_id_type=MESH
            )

    pl.semaphore_wait(barrier, present)

    def copy(i):
        rows, cols = DIRECTIONS[i]
        return pltpu.make_async_remote_copy(
            sources[i], outs[i], send.at[i], recv.at[i], (y + rows, x + cols), MESH
        )

    for i, (rows, cols) in enumerate(DIRECTIONS):

        @pl.when(inside(rows, cols))
        def _():
            copy(i).start()

    for i, (rows, cols) in enumerate(DIRECTIONS):
        arrives = inside(-rows, -cols)

        @pl.when(arrives)
        def _():
            copy(i).wait_recv()

        @pl.when(jnp.logical_not(arrives))
        def _():
            outs[i][...] = jnp.zeros_like(outs[i])

    for i, (rows, cols) in enumerate(DIRECTIONS):

        @pl.when(inside(rows, cols))
        def _():
            copy(i).wait_send()


def halos(radiance, collective_id):
    height, width, channels = radiance.shape
    n_gy, n_gx = lax.axis_size("gy"), lax.axis_size("gx")
    first, last = radiance[:, 0], radiance[:, width - 1]
    corners = jnp.stack([last[height - 1], first[height - 1], last[0], first[0]])
    corners = corners.reshape(4, 16, channels // 16)
    shapes = [(width, channels)] * 2 + [(height, channels)] * 2 + [(16, channels // 16)] * 4
    vmem = pl.BlockSpec(memory_space=pltpu.VMEM)
    outs = pl.pallas_call(
        functools.partial(halo_kernel, n_gy, n_gx),
        out_shape=[jax.ShapeDtypeStruct(shape, radiance.dtype) for shape in shapes],
        in_specs=[pl.BlockSpec(memory_space=pl.ANY), vmem, vmem, vmem],
        out_specs=[vmem] * 8,
        scratch_shapes=[pltpu.SemaphoreType.DMA((8,)), pltpu.SemaphoreType.DMA((8,))],
        compiler_params=pltpu.CompilerParams(collective_id=collective_id, has_side_effects=True),
        name="halo",
    )(radiance, first, last, corners)
    return outs[:4], jnp.stack(outs[4:]).reshape(4, channels)


def smooth_kernel(
    x_ref, up_ref, down_ref, left_ref, right_ref, c_ref, k_ref, t_ref, o_ref, s_ref, side, l_s, r_s
):
    height, width, block = x_ref.shape

    @pl.when(pl.program_id(0) == 0)
    def _():
        s_ref[...] = jnp.zeros_like(s_ref)

    for part in range(block // LANES):
        lanes = pl.ds(part * LANES, LANES)
        k = [[k_ref[pl.ds(3 * a + b, 1), lanes] for b in range(3)] for a in range(3)]
        corners = c_ref[:, lanes].astype(jnp.float32)
        for b, middle, corner, sums in ((0, left_ref, 0, l_s), (2, right_ref, 1, r_s)):
            side[pl.ds(8, height), :] = middle[:, lanes].astype(jnp.float32)
            side[pl.ds(7, 1), :] = corners[corner : corner + 1]
            side[pl.ds(8 + height, 1), :] = corners[corner + 2 : corner + 3]
            sums[...] = sum(k[a][b] * side[pl.ds(7 + a, height), :] for a in range(3))
        place = lax.broadcasted_iota(jnp.int32, (width, LANES), 0)

        def row_out(h, above, here, below):
            p = [k[0][b] * above + k[1][b] * here + k[2][b] * below for b in range(3)]
            before = jnp.where(place == 0, l_s[pl.ds(h, 1), :], pltpu.roll(p[0], 1, 0))
            after = jnp.where(place == width - 1, r_s[pl.ds(h, 1), :], pltpu.roll(p[2], width - 1, 0))
            o_ref[h, :, lanes] = (p[1] + before + after).astype(jnp.bfloat16)

        def step(h, carry):
            above, here = carry
            below = x_ref[h + 1, :, lanes].astype(jnp.float32)
            row_out(h, above, here, below)
            return here, below

        first = (up_ref[:, lanes].astype(jnp.float32), x_ref[0, :, lanes].astype(jnp.float32))
        above, here = lax.fori_loop(0, height - 1, step, first, unroll=3)
        row_out(height - 1, above, here, down_ref[:, lanes].astype(jnp.float32))

    s_ref[...] += jnp.dot(
        o_ref[...].reshape(height * width, block), t_ref[...], preferred_element_type=jnp.float32
    )


def smooth_and_sketch(radiance, kernel, test_matrix):
    height, width, channels = radiance.shape
    k_width = test_matrix.shape[1]
    block = 512
    (up, down, left, right), corners = halos(radiance, 4)
    pixels = height * width
    return pl.pallas_call(
        smooth_kernel,
        grid=(channels // block,),
        in_specs=[
            pl.BlockSpec((height, width, block), lambda i: (0, 0, i)),
            pl.BlockSpec((width, block), lambda i: (0, i)),
            pl.BlockSpec((width, block), lambda i: (0, i)),
            pl.BlockSpec((height, block), lambda i: (0, i)),
            pl.BlockSpec((height, block), lambda i: (0, i)),
            pl.BlockSpec((4, block), lambda i: (0, i)),
            pl.BlockSpec((9, block), lambda i: (0, i)),
            pl.BlockSpec((block, k_width), lambda i: (i, 0)),
        ],
        out_specs=[
            pl.BlockSpec((height, width, block), lambda i: (0, 0, i)),
            pl.BlockSpec((pixels, k_width), lambda i: (0, 0)),
        ],
        out_shape=[
            jax.ShapeDtypeStruct((height, width, channels), jnp.bfloat16),
            jax.ShapeDtypeStruct((pixels, k_width), jnp.float32),
        ],
        scratch_shapes=[
            pltpu.VMEM((height + 16, LANES), jnp.float32),
            pltpu.VMEM((height, LANES), jnp.float32),
            pltpu.VMEM((height, LANES), jnp.float32),
        ],
        compiler_params=pltpu.CompilerParams(vmem_limit_bytes=VMEM_LIMIT),
        cost_estimate=pl.CostEstimate(
            flops=pixels * channels * (2 * k_width + 18),
            bytes_accessed=4 * pixels * channels,
            transcendentals=0,
        ),
        name="smooth_sketch",
    )(radiance, up, down, left, right, corners, kernel.reshape(9, channels), test_matrix)


def tree_sum(values):
    while len(values) > 1:
        values = [values[i] + values[i + 1] for i in range(0, len(values), 2)]
    return values[0]


def gram_kernel(n_gy, n_gx, x_ref, o_ref, recv_x, recv_y, mine, sx, rx, sy, ry, sg, rg):
    bits_x, bits_y = n_gx.bit_length() - 1, n_gy.bit_length() - 1
    me_x, me_y = lax.axis_index("gx"), lax.axis_index("gy")
    rows = x_ref.shape[0] // n_gx
    along_x = [flipped(me_x, d, bits_x) for d in range(n_gx)]
    along_y = [flipped(me_y, d, bits_y) for d in range(n_gy)]
    greet([(me_y, p) for p in along_x[1:]] + [(p, me_x) for p in along_y[1:]])

    def block(ref, index):
        return ref.at[pl.ds(pl.multiple_of(index * rows, rows), rows), :]

    copies = []
    for d in range(1, n_gx):
        copy = pltpu.make_async_remote_copy(
            block(x_ref, along_x[d]), recv_x.at[d], sx.at[d], rx.at[d], (me_y, along_x[d]), MESH
        )
        copy.start()
        copies.append(copy)
    for copy in copies:
        copy.wait_recv()
    own = x_ref[pl.ds(pl.multiple_of(me_x * rows, rows), rows), :]
    mine[...] = tree_sum([own] + [recv_x[d] for d in range(1, n_gx)])
    later = []
    for d in range(1, n_gy):
        copy = pltpu.make_async_remote_copy(
            mine, recv_y.at[d], sy.at[d], ry.at[d], (along_y[d], me_x), MESH
        )
        copy.start()
        later.append(copy)
    for copy in later:
        copy.wait_recv()
    total = tree_sum([mine[...]] + [recv_y[d] for d in range(1, n_gy)])
    o_ref[pl.ds(pl.multiple_of(me_x * rows, rows), rows), :] = total
    last = []
    for d in range(1, n_gx):
        copy = pltpu.make_async_remote_copy(
            block(o_ref, me_x), block(o_ref, me_x), sg.at[d], rg.at[d], (me_y, along_x[d]), MESH
        )
        copy.start()
        last.append(copy)
    for d in range(1, n_gx):
        pltpu.make_async_remote_copy(
            block(o_ref, along_x[d]), block(o_ref, along_x[d]), sg.at[d], rg.at[d], (me_y, along_x[d]), MESH
        ).wait_recv()
    for copy in copies + later + last:
        copy.wait_send()


def summed_gram(gram, collective_id):
    n_gy, n_gx = lax.axis_size("gy"), lax.axis_size("gx")
    k = gram.shape[0]
    rows = k // n_gx
    dma = pltpu.SemaphoreType.DMA
    return pl.pallas_call(
        functools.partial(gram_kernel, n_gy, n_gx),
        out_shape=jax.ShapeDtypeStruct(gram.shape, jnp.float32),
        in_specs=[pl.BlockSpec(memory_space=pltpu.VMEM)],
        out_specs=pl.BlockSpec(memory_space=pltpu.VMEM),
        scratch_shapes=[
            pltpu.VMEM((n_gx, rows, k), jnp.float32),
            pltpu.VMEM((n_gy, rows, k), jnp.float32),
            pltpu.VMEM((rows, k), jnp.float32),
            dma((n_gx,)),
            dma((n_gx,)),
            dma((n_gy,)),
            dma((n_gy,)),
            dma((n_gx,)),
            dma((n_gx,)),
        ],
        compiler_params=pltpu.CompilerParams(collective_id=collective_id, has_side_effects=True),
        name="gram_sum",
    )(gram)


def wide_orders(n_gy, n_gx, chunks):
    x_steps = [("gx", b, 1) for b in range(n_gx.bit_length() - 1)]
    y_bits = n_gy.bit_length() - 1
    y_steps = [("gy", b, 1) for b in range(max(y_bits - 2, 0))]
    if y_bits >= 2:
        y_steps.append(("gy", y_bits - 2, 2))
    elif y_bits:
        y_steps.append(("gy", 0, 1))
    first, across = x_steps[:1], x_steps[1:]
    return [first + (across[::-1] if q % 2 else across) + y_steps for q in range(chunks)]


def kept_shapes(rows, cols, order):
    shapes = []
    for _, _, bits in order:
        if rows >= 16 * 2**bits:
            rows //= 2**bits
        else:
            cols //= 2**bits
        shapes.append((rows, cols))
    return shapes


def wide_kernel(orders, blocks, again, b_ref, f_ref, *rest):
    o_ref, work, held, load = rest[:4]
    rest = rest[4:]
    gathered = o_ref
    if again:
        gathered, rest = rest[0], rest[1:]
    steps, chunks = len(orders[0]), len(orders)
    recv = [rest[q * steps : (q + 1) * steps] for q in range(chunks)]
    s_send, s_recv, g_send, g_recv = rest[chunks * steps :]
    rows, cols = work.shape
    wide = cols // chunks
    block = cols // blocks
    me = {"gx": lax.axis_index("gx"), "gy": lax.axis_index("gy")}

    def partner(step, d):
        axis, bit, bits = step
        other = dict(me)
        other[axis] = flipped(me[axis], d << bit, bit + bits)
        return (other["gy"], other["gx"])

    loads = [
        pltpu.make_async_copy(f_ref.at[:, pl.ds(i * block, block)], held.at[i], load.at[i])
        for i in range(blocks)
    ]
    for copy in loads:
        copy.start()
    barrier = pltpu.get_barrier_semaphore()
    others = [partner(step, d) for step in orders[0] for d in range(1, 2 ** step[2])]
    for other in others:
        pl.semaphore_signal(barrier, inc=1, device_id=other, device_id_type=MESH)

    places, shapes, index, count = [], [], [], 0
    for q in range(chunks):
        row, col, size = 0, q * wide, (rows, wide)
        shapes.append(kept_shapes(rows, wide, orders[q]))
        places.append([])
        index.append([])
        for s, (axis, bit, bits) in enumerate(orders[q]):
            h, w = shapes[q][s]
            at = []
            for d in range(2**bits):
                part = flipped((me[axis] // 2**bit) % 2**bits, d, bits)
                at.append((row + part * h, col) if h < size[0] else (row, col + part * w))
            places[q].append(at)
            index[q].append(count - 1)
            count += 2**bits - 1
            row, col = at[0]
            size = (h, w)

    def region(q, s, d):
        (row, col), shape = places[q][s][d], shapes[q][s]
        row = row if isinstance(row, int) else pl.multiple_of(row, 16)
        col = col if isinstance(col, int) else pl.multiple_of(col, LANES)
        return (pl.ds(row, shape[0]), pl.ds(col, shape[1]))

    def reduce_copies(q, s):
        copies = []
        for d in range(1, 2 ** orders[q][s][2]):
            sem = index[q][s] + d
            copies.append(
                pltpu.make_async_remote_copy(
                    work.at[region(q, s, d)],
                    recv[q][s].at[d - 1],
                    s_send.at[sem],
                    s_recv.at[sem],
                    partner(orders[q][s], d),
                    MESH,
                )
            )
        return copies

    def gather_copies(q, s, outgoing):
        copies = []
        for d in range(1, 2 ** orders[q][s][2]):
            sem = index[q][s] + d
            at = gathered.at[region(q, s, 0 if outgoing else d)]
            copies.append(
                pltpu.make_async_remote_copy(
                    at, at, g_send.at[sem], g_recv.at[sem], partner(orders[q][s], d), MESH
                )
            )
        return copies

    def start(copies):
        for copy in copies:
            copy.start()

    def advance(q, stage):
        if stage < steps:
            s = stage
            for copy in reduce_copies(q, s):
                copy.wait_recv()
            here = region(q, s, 0)
            parts = [work[here]] + [recv[q][s][d - 1] for d in range(1, 2 ** orders[q][s][2])]
            total = tree_sum(parts)
            if s + 1 < steps:
                work[here] = total
                start(reduce_copies(q, s + 1))
            else:
                gathered[here] = total.astype(gathered.dtype)
                start(gather_copies(q, s, True))
            return
        s = 2 * steps - 1 - stage
        for copy in gather_copies(q, s, False):
            copy.wait_recv()
        if s > 0:
            start(gather_copies(q, s - 1, True))
        elif again:
            per = wide // block
            for i in range(q * per, (q + 1) * per):
                part = lax.dot_general(
                    held[i],
                    gathered[:, i * block : (i + 1) * block],
                    (((1,), (1,)), ((), ())),
                    preferred_element_type=jnp.float32,
                )
                o_ref[...] = part if i == 0 else o_ref[...] + part

    stages = [0] * chunks
    for q in range(chunks):
        per = wide // block
        for i in range(q * per, (q + 1) * per):
            loads[i].wait()
            work[:, i * block : (i + 1) * block] = jnp.dot(
                b_ref[...], held[i], preferred_element_type=jnp.float32
            )
        if q == 0:
            pl.semaphore_wait(barrier, len(others))
        start(reduce_copies(q, 0))
        for p in range(q):
            advance(p, stages[p])
            stages[p] += 1
    while min(stages) < 2 * steps:
        for q in range(chunks):
            if stages[q] < 2 * steps:
                advance(q, stages[q])
                stages[q] += 1
    for q in range(chunks):
        for s in range(steps):
            for copy in reduce_copies(q, s) + gather_copies(q, s, True):
                copy.wait_send()


def wide_product(basis, flattened, collective_id, again):
    n_gy, n_gx = lax.axis_size("gy"), lax.axis_size("gx")
    pixels, cols = flattened.shape
    rows = basis.shape[1]
    chunks = min(4, rows * cols // (16 * LANES * n_gy * n_gx))
    blocks = 8
    orders = wide_orders(n_gy, n_gx, chunks)
    shapes = [kept_shapes(rows, cols // chunks, order) for order in orders]
    copies = chunks * sum(2**bits - 1 for _, _, bits in orders[0])
    dma = pltpu.SemaphoreType.DMA
    scratch = [
        pltpu.VMEM((rows, cols), jnp.float32),
        pltpu.VMEM((blocks, pixels, cols // blocks), jnp.bfloat16),
        dma((blocks,)),
    ]
    if again:
        scratch.append(pltpu.VMEM((rows, cols), jnp.bfloat16))
    for order, of_chunk in zip(orders, shapes):
        for (_, _, bits), shape in zip(order, of_chunk):
            scratch.append(pltpu.VMEM((2**bits - 1, *shape), jnp.float32))
    vmem = pl.BlockSpec(memory_space=pltpu.VMEM)
    return pl.pallas_call(
        functools.partial(wide_kernel, orders, blocks, again),
        out_shape=jax.ShapeDtypeStruct((pixels, rows) if again else (rows, cols), jnp.float32),
        in_specs=[vmem, pl.BlockSpec(memory_space=pl.ANY)],
        out_specs=vmem,
        scratch_shapes=scratch + [dma((copies,))] * 4,
        compiler_params=pltpu.CompilerParams(
            collective_id=collective_id, has_side_effects=True, vmem_limit_bytes=VMEM_LIMIT
        ),
        name="wide_product",
    )(basis.T, flattened)


def inverse_factor_kernel(gram_ref, o_ref, state):
    size = gram_ref.shape[0]
    row = lax.broadcasted_iota(jnp.int32, (size, size), 0)
    col = lax.broadcasted_iota(jnp.int32, (size, size), 1)
    state[:, :size] = gram_ref[...]
    state[:, size:] = jnp.where(row == col, 1.0, 0.0)
    shape = (8, size)
    place = lax.broadcasted_iota(jnp.int32, shape, 0)
    for start in range(0, size, 8):
        left = state[start : start + 8, :size]
        right = state[start : start + 8, size:]
        columns = [
            jnp.broadcast_to(left[:, start + j : start + j + 1], shape) for j in range(8)
        ]
        scale = jnp.zeros(shape, jnp.float32)
        for j in range(8):

            def pivot_row(value):
                return jnp.broadcast_to(value[j : j + 1], shape)

            inverse = 1.0 / pivot_row(columns[j])
            scale = jnp.where(place == j, inverse, scale)
            if j == 7:
                break
            factor = jnp.where(place > j, columns[j] * inverse, 0.0)
            left = left - factor * pivot_row(left)
            right = right - factor * pivot_row(right)
            for i in range(j + 1, 8):
                columns[i] = columns[i] - factor * pivot_row(columns[i])
        o_ref[start : start + 8, :] = right * jnp.sqrt(scale)
        if start + 8 < size:
            update = jnp.dot(
                (left * scale).T,
                jnp.concatenate([left, right], axis=1),
                precision=lax.Precision.HIGHEST,
                preferred_element_type=jnp.float32,
            )
            state[start + 8 :, :] = state[start + 8 :, :] - update[start + 8 :, :]


def inverse_factor(gram):
    size = gram.shape[0]
    return pl.pallas_call(
        inverse_factor_kernel,
        out_shape=jax.ShapeDtypeStruct(gram.shape, jnp.float32),
        in_specs=[pl.BlockSpec(memory_space=pltpu.VMEM)],
        out_specs=pl.BlockSpec(memory_space=pltpu.VMEM),
        scratch_shapes=[pltpu.VMEM((size, 2 * size), jnp.float32)],
        name="inverse_factor",
    )(gram)


def factor_basis(values, collective_id):
    local_gram = jnp.dot(
        values.T, values, precision=lax.Precision.HIGHEST, preferred_element_type=jnp.float32
    )
    inverse = inverse_factor(summed_gram(local_gram, collective_id))
    return jnp.dot(
        values, inverse.T, precision=lax.Precision.HIGHEST, preferred_element_type=jnp.float32
    )


def on_device(radiance, kernel, test_matrix):
    height, breadth, channels = radiance.shape
    devices = lax.axis_size("gy") * lax.axis_size("gx")
    pixel_count = height * breadth * devices
    smoothed, sketch = smooth_and_sketch(radiance, kernel, test_matrix)
    flattened = smoothed.reshape(height * breadth, channels)
    first_basis = factor_basis(sketch, 0).astype(jnp.bfloat16)
    second = wide_product(first_basis, flattened, 2, True)
    basis_out = factor_basis(second, 1) * math.sqrt(pixel_count)
    basis_half = basis_out.astype(jnp.bfloat16)
    projected = wide_product(basis_half, flattened, 3, False)
    coeffs = projected * (math.sqrt(channels) / pixel_count)
    return (basis_out.reshape(height, breadth, basis_out.shape[1]), coeffs)


def solution(mesh):
    placed = (P("gy", "gx", None), P(), P())
    return jax.shard_map(
        on_device, mesh=mesh, in_specs=placed, out_specs=(P("gy", "gx", None), P()), check_vma=False
    )
```

```python
import functools
import math

import jax
import jax.numpy as jnp
from jax import lax
from jax.experimental import pallas as pl
from jax.experimental.pallas import tpu as pltpu
from jax.sharding import PartitionSpec as P

MESH = pl.DeviceIdType.MESH
LANES = 128
VMEM_LIMIT = 56 * 1024 * 1024


def bit_of(index, bit):
    return (index // 2**bit) % 2


def flipped(index, mask, bits):
    for bit in range(bits):
        if (mask >> bit) & 1:
            index = index + 2**bit * (1 - 2 * bit_of(index, bit))
    return index


def greet(partners):
    barrier = pltpu.get_barrier_semaphore()
    for partner in partners:
        pl.semaphore_signal(barrier, inc=1, device_id=partner, device_id_type=MESH)
    pl.semaphore_wait(barrier, len(partners))


DIRECTIONS = ((1, 0), (-1, 0), (0, 1), (0, -1), (1, 1), (1, -1), (-1, 1), (-1, -1))


def halo_kernel(n_gy, n_gx, x_ref, first_ref, last_ref, c0, c1, c2, c3, *rest):
    outs, (send, recv) = rest[:8], rest[8:]
    height = x_ref.shape[0]
    y, x = lax.axis_index("gy"), lax.axis_index("gx")
    sources = [x_ref.at[height - 1], x_ref.at[0], last_ref, first_ref, c0, c1, c2, c3]
    barrier = pltpu.get_barrier_semaphore()

    def inside(rows, cols):
        return (y + rows >= 0) & (y + rows < n_gy) & (x + cols >= 0) & (x + cols < n_gx)

    present = 0
    for rows, cols in DIRECTIONS:
        there = inside(rows, cols)
        present = present + jnp.where(there, 1, 0)

        @pl.when(there)
        def _():
            pl.semaphore_signal(
                barrier, inc=1, device_id=(y + rows, x + cols), device_id_type=MESH
            )

    pl.semaphore_wait(barrier, present)

    def copy(i):
        rows, cols = DIRECTIONS[i]
        return pltpu.make_async_remote_copy(
            sources[i], outs[i], send.at[i], recv.at[i], (y + rows, x + cols), MESH
        )

    for i, (rows, cols) in enumerate(DIRECTIONS):

        @pl.when(inside(rows, cols))
        def _():
            copy(i).start()

    for i, (rows, cols) in enumerate(DIRECTIONS):
        arrives = inside(-rows, -cols)

        @pl.when(arrives)
        def _():
            copy(i).wait_recv()

        @pl.when(jnp.logical_not(arrives))
        def _():
            outs[i][...] = jnp.zeros_like(outs[i])

    for i, (rows, cols) in enumerate(DIRECTIONS):

        @pl.when(inside(rows, cols))
        def _():
            copy(i).wait_send()


def halos(radiance, collective_id):
    height, width, channels = radiance.shape
    n_gy, n_gx = lax.axis_size("gy"), lax.axis_size("gx")
    first, last = radiance[:, 0], radiance[:, width - 1]
    corners = [
        radiance[row : row + 1, col].astype(jnp.float32)
        for row in (height - 1, 0)
        for col in (width - 1, 0)
    ]
    shapes = [(width, channels)] * 2 + [(height, channels)] * 2 + [(1, channels)] * 4
    kinds = [radiance.dtype] * 4 + [jnp.float32] * 4
    vmem = pl.BlockSpec(memory_space=pltpu.VMEM)
    outs = pl.pallas_call(
        functools.partial(halo_kernel, n_gy, n_gx),
        out_shape=[jax.ShapeDtypeStruct(*each) for each in zip(shapes, kinds)],
        in_specs=[pl.BlockSpec(memory_space=pl.ANY)] + [vmem] * 6,
        out_specs=[vmem] * 8,
        scratch_shapes=[pltpu.SemaphoreType.DMA((8,)), pltpu.SemaphoreType.DMA((8,))],
        compiler_params=pltpu.CompilerParams(collective_id=collective_id, has_side_effects=True),
        name="halo",
    )(radiance, first, last, *corners)
    return outs


def smooth_kernel(
    x_ref, up_ref, down_ref, left_ref, right_ref, c0, c1, c2, c3, k_ref, t_ref, o_ref, s_ref, flat
):
    height, width, block = x_ref.shape
    pitch = width + 8

    @pl.when(pl.program_id(0) == 0)
    def _():
        s_ref[...] = jnp.zeros_like(s_ref)

    for part in range(block // LANES):
        lanes = pl.ds(part * LANES, LANES)

        def fill(h, carry):
            flat[pl.ds(pl.multiple_of((h + 1) * pitch + 8, 8), width), :] = x_ref[h, :, lanes].astype(
                jnp.float32
            )
            return carry

        lax.fori_loop(0, height, fill, 0, unroll=8)
        flat[pl.ds(8, width), :] = up_ref[:, lanes].astype(jnp.float32)
        flat[pl.ds((height + 1) * pitch + 8, width), :] = down_ref[:, lanes].astype(jnp.float32)
        flat[pl.ds(pitch + 7, height, stride=pitch), :] = left_ref[:, lanes].astype(jnp.float32)
        flat[pl.ds(2 * pitch, height, stride=pitch), :] = right_ref[:, lanes].astype(jnp.float32)
        flat[pl.ds(7, 1), :] = c0[:, lanes]
        flat[pl.ds(pitch, 1), :] = c1[:, lanes]
        flat[pl.ds((height + 1) * pitch + 7, 1), :] = c2[:, lanes]
        flat[pl.ds((height + 2) * pitch, 1), :] = c3[:, lanes]
        k = [
            [jnp.broadcast_to(k_ref[a, pl.ds(b, 1), lanes], (16, LANES)) for b in range(3)]
            for a in range(3)
        ]
        for first in range(0, width, 16):

            def shifts(h):
                start = pl.multiple_of(h * pitch, 8) + 7 + first
                return [flat[pl.ds(start + b, 16), :] for b in range(3)]

            def step(h, carry):
                above, here = carry
                below = shifts(h + 2)
                total = [
                    k[0][b] * above[b] + k[1][b] * here[b] + k[2][b] * below[b] for b in range(3)
                ]
                o_ref[h, pl.ds(first, 16), lanes] = (total[0] + total[1] + total[2]).astype(
                    jnp.bfloat16
                )
                return here, below

            lax.fori_loop(0, height, step, (shifts(0), shifts(1)), unroll=8)

    s_ref[...] += jnp.dot(
        o_ref[...].reshape(height * width, block), t_ref[...], preferred_element_type=jnp.float32
    )


def smooth_and_sketch(radiance, kernel, test_matrix):
    height, width, channels = radiance.shape
    k_width = test_matrix.shape[1]
    block = 512
    border = halos(radiance, 4)
    pixels = height * width
    return pl.pallas_call(
        smooth_kernel,
        grid=(channels // block,),
        in_specs=[
            pl.BlockSpec((height, width, block), lambda i: (0, 0, i)),
            pl.BlockSpec((width, block), lambda i: (0, i)),
            pl.BlockSpec((width, block), lambda i: (0, i)),
            pl.BlockSpec((height, block), lambda i: (0, i)),
            pl.BlockSpec((height, block), lambda i: (0, i)),
        ]
        + [pl.BlockSpec((1, block), lambda i: (0, i))] * 4
        + [
            pl.BlockSpec((3, 3, block), lambda i: (0, 0, i)),
            pl.BlockSpec((block, k_width), lambda i: (i, 0)),
        ],
        out_specs=[
            pl.BlockSpec((height, width, block), lambda i: (0, 0, i)),
            pl.BlockSpec((pixels, k_width), lambda i: (0, 0)),
        ],
        out_shape=[
            jax.ShapeDtypeStruct((height, width, channels), jnp.bfloat16),
            jax.ShapeDtypeStruct((pixels, k_width), jnp.float32),
        ],
        scratch_shapes=[
            pltpu.VMEM(((height + 3) * (width + 8), LANES), jnp.float32),
        ],
        compiler_params=pltpu.CompilerParams(vmem_limit_bytes=VMEM_LIMIT),
        cost_estimate=pl.CostEstimate(
            flops=pixels * channels * (2 * k_width + 18),
            bytes_accessed=4 * pixels * channels,
            transcendentals=0,
        ),
        name="smooth_sketch",
    )(radiance, *border, kernel, test_matrix)


def tree_sum(values):
    while len(values) > 1:
        values = [values[i] + values[i + 1] for i in range(0, len(values), 2)]
    return values[0]


def gram_kernel(n_gy, n_gx, x_ref, o_ref, recv_x, recv_y, mine, sx, rx, sy, ry, sg, rg):
    bits_x, bits_y = n_gx.bit_length() - 1, n_gy.bit_length() - 1
    me_x, me_y = lax.axis_index("gx"), lax.axis_index("gy")
    rows = x_ref.shape[0] // n_gx
    along_x = [flipped(me_x, d, bits_x) for d in range(n_gx)]
    along_y = [flipped(me_y, d, bits_y) for d in range(n_gy)]
    greet([(me_y, p) for p in along_x[1:]] + [(p, me_x) for p in along_y[1:]])

    def block(ref, index):
        return ref.at[pl.ds(pl.multiple_of(index * rows, rows), rows), :]

    copies = []
    for d in range(1, n_gx):
        copy = pltpu.make_async_remote_copy(
            block(x_ref, along_x[d]), recv_x.at[d], sx.at[d], rx.at[d], (me_y, along_x[d]), MESH
        )
        copy.start()
        copies.append(copy)
    for copy in copies:
        copy.wait_recv()
    own = x_ref[pl.ds(pl.multiple_of(me_x * rows, rows), rows), :]
    mine[...] = tree_sum([own] + [recv_x[d] for d in range(1, n_gx)])
    later = []
    for d in range(1, n_gy):
        copy = pltpu.make_async_remote_copy(
            mine, recv_y.at[d], sy.at[d], ry.at[d], (along_y[d], me_x), MESH
        )
        copy.start()
        later.append(copy)
    for copy in later:
        copy.wait_recv()
    total = tree_sum([mine[...]] + [recv_y[d] for d in range(1, n_gy)])
    o_ref[pl.ds(pl.multiple_of(me_x * rows, rows), rows), :] = total
    last = []
    for d in range(1, n_gx):
        copy = pltpu.make_async_remote_copy(
            block(o_ref, me_x), block(o_ref, me_x), sg.at[d], rg.at[d], (me_y, along_x[d]), MESH
        )
        copy.start()
        last.append(copy)
    for d in range(1, n_gx):
        pltpu.make_async_remote_copy(
            block(o_ref, along_x[d]), block(o_ref, along_x[d]), sg.at[d], rg.at[d], (me_y, along_x[d]), MESH
        ).wait_recv()
    for copy in copies + later + last:
        copy.wait_send()


def summed_gram(gram, collective_id):
    n_gy, n_gx = lax.axis_size("gy"), lax.axis_size("gx")
    k = gram.shape[0]
    rows = k // n_gx
    dma = pltpu.SemaphoreType.DMA
    return pl.pallas_call(
        functools.partial(gram_kernel, n_gy, n_gx),
        out_shape=jax.ShapeDtypeStruct(gram.shape, jnp.float32),
        in_specs=[pl.BlockSpec(memory_space=pltpu.VMEM)],
        out_specs=pl.BlockSpec(memory_space=pltpu.VMEM),
        scratch_shapes=[
            pltpu.VMEM((n_gx, rows, k), jnp.float32),
            pltpu.VMEM((n_gy, rows, k), jnp.float32),
            pltpu.VMEM((rows, k), jnp.float32),
            dma((n_gx,)),
            dma((n_gx,)),
            dma((n_gy,)),
            dma((n_gy,)),
            dma((n_gx,)),
            dma((n_gx,)),
        ],
        compiler_params=pltpu.CompilerParams(collective_id=collective_id, has_side_effects=True),
        name="gram_sum",
    )(gram)


def wide_orders(n_gy, n_gx, chunks):
    x_steps = [("gx", b, 1) for b in range(n_gx.bit_length() - 1)]
    y_bits = n_gy.bit_length() - 1
    y_steps = [("gy", b, 1) for b in range(max(y_bits - 2, 0))]
    if y_bits >= 2:
        y_steps.append(("gy", y_bits - 2, 2))
    elif y_bits:
        y_steps.append(("gy", 0, 1))
    first, across = x_steps[:1], x_steps[1:]
    return [first + (across[::-1] if q % 2 else across) + y_steps for q in range(chunks)]


def kept_shapes(rows, cols, order):
    shapes = []
    for _, _, bits in order:
        if rows >= 16 * 2**bits:
            rows //= 2**bits
        else:
            cols //= 2**bits
        shapes.append((rows, cols))
    return shapes


def wide_kernel(orders, blocks, again, scale, b_ref, f_ref, *rest):
    o_ref, work, held, load = rest[:4]
    rest = rest[4:]
    gathered = o_ref
    if again:
        gathered, rest = rest[0], rest[1:]
    steps, chunks = len(orders[0]), len(orders)
    recv = [rest[q * steps : (q + 1) * steps] for q in range(chunks)]
    s_send, s_recv, g_send, g_recv = rest[chunks * steps :]
    rows, cols = work.shape
    wide = cols // chunks
    block = cols // blocks
    me = {"gx": lax.axis_index("gx"), "gy": lax.axis_index("gy")}

    def partner(step, d):
        axis, bit, bits = step
        other = dict(me)
        other[axis] = flipped(me[axis], d << bit, bit + bits)
        return (other["gy"], other["gx"])

    loads = [
        pltpu.make_async_copy(f_ref.at[:, pl.ds(i * block, block)], held.at[i], load.at[i])
        for i in range(blocks)
    ]
    for copy in loads:
        copy.start()
    barrier = pltpu.get_barrier_semaphore()
    others = [partner(step, d) for step in orders[0] for d in range(1, 2 ** step[2])]
    for other in others:
        pl.semaphore_signal(barrier, inc=1, device_id=other, device_id_type=MESH)

    places, shapes, index, count = [], [], [], 0
    for q in range(chunks):
        row, col, size = 0, q * wide, (rows, wide)
        shapes.append(kept_shapes(rows, wide, orders[q]))
        places.append([])
        index.append([])
        for s, (axis, bit, bits) in enumerate(orders[q]):
            h, w = shapes[q][s]
            at = []
            for d in range(2**bits):
                part = flipped((me[axis] // 2**bit) % 2**bits, d, bits)
                at.append((row + part * h, col) if h < size[0] else (row, col + part * w))
            places[q].append(at)
            index[q].append(count - 1)
            count += 2**bits - 1
            row, col = at[0]
            size = (h, w)

    def region(q, s, d):
        (row, col), shape = places[q][s][d], shapes[q][s]
        row = row if isinstance(row, int) else pl.multiple_of(row, 16)
        col = col if isinstance(col, int) else pl.multiple_of(col, LANES)
        return (pl.ds(row, shape[0]), pl.ds(col, shape[1]))

    def reduce_copies(q, s):
        copies = []
        for d in range(1, 2 ** orders[q][s][2]):
            sem = index[q][s] + d
            copies.append(
                pltpu.make_async_remote_copy(
                    work.at[region(q, s, d)],
                    recv[q][s].at[d - 1],
                    s_send.at[sem],
                    s_recv.at[sem],
                    partner(orders[q][s], d),
                    MESH,
                )
            )
        return copies

    def gather_copies(q, s, outgoing):
        copies = []
        for d in range(1, 2 ** orders[q][s][2]):
            sem = index[q][s] + d
            at = gathered.at[region(q, s, 0 if outgoing else d)]
            copies.append(
                pltpu.make_async_remote_copy(
                    at, at, g_send.at[sem], g_recv.at[sem], partner(orders[q][s], d), MESH
                )
            )
        return copies

    def start(copies):
        for copy in copies:
            copy.start()

    def advance(q, stage):
        if stage < steps:
            s = stage
            for copy in reduce_copies(q, s):
                copy.wait_recv()
            here = region(q, s, 0)
            parts = [work[here]] + [recv[q][s][d - 1] for d in range(1, 2 ** orders[q][s][2])]
            total = tree_sum(parts)
            if s + 1 < steps:
                work[here] = total
                start(reduce_copies(q, s + 1))
            else:
                gathered[here] = (total * scale).astype(gathered.dtype)
                start(gather_copies(q, s, True))
            return
        s = 2 * steps - 1 - stage
        for copy in gather_copies(q, s, False):
            copy.wait_recv()
        if s > 0:
            start(gather_copies(q, s - 1, True))
        elif again:
            per = wide // block
            for i in range(q * per, (q + 1) * per):
                part = lax.dot_general(
                    held[i],
                    gathered[:, i * block : (i + 1) * block],
                    (((1,), (1,)), ((), ())),
                    preferred_element_type=jnp.float32,
                )
                o_ref[...] = part if i == 0 else o_ref[...] + part

    stages = [0] * chunks
    for q in range(chunks):
        per = wide // block
        for i in range(q * per, (q + 1) * per):
            loads[i].wait()
            work[:, i * block : (i + 1) * block] = jnp.dot(
                b_ref[...], held[i], preferred_element_type=jnp.float32
            )
        if q == 0:
            pl.semaphore_wait(barrier, len(others))
        start(reduce_copies(q, 0))
        for p in range(q):
            advance(p, stages[p])
            stages[p] += 1
    while min(stages) < 2 * steps:
        for q in range(chunks):
            if stages[q] < 2 * steps:
                advance(q, stages[q])
                stages[q] += 1
    for q in range(chunks):
        for s in range(steps):
            for copy in reduce_copies(q, s) + gather_copies(q, s, True):
                copy.wait_send()


def wide_product(basis, flattened, collective_id, again, scale):
    n_gy, n_gx = lax.axis_size("gy"), lax.axis_size("gx")
    pixels, cols = flattened.shape
    rows = basis.shape[1]
    chunks = min(4, rows * cols // (16 * LANES * n_gy * n_gx))
    blocks = 8
    orders = wide_orders(n_gy, n_gx, chunks)
    shapes = [kept_shapes(rows, cols // chunks, order) for order in orders]
    copies = chunks * sum(2**bits - 1 for _, _, bits in orders[0])
    dma = pltpu.SemaphoreType.DMA
    scratch = [
        pltpu.VMEM((rows, cols), jnp.float32),
        pltpu.VMEM((blocks, pixels, cols // blocks), jnp.bfloat16),
        dma((blocks,)),
    ]
    if again:
        scratch.append(pltpu.VMEM((rows, cols), jnp.bfloat16))
    for order, of_chunk in zip(orders, shapes):
        for (_, _, bits), shape in zip(order, of_chunk):
            scratch.append(pltpu.VMEM((2**bits - 1, *shape), jnp.float32))
    vmem = pl.BlockSpec(memory_space=pltpu.VMEM)
    return pl.pallas_call(
        functools.partial(wide_kernel, orders, blocks, again, scale),
        out_shape=jax.ShapeDtypeStruct((pixels, rows) if again else (rows, cols), jnp.float32),
        in_specs=[vmem, pl.BlockSpec(memory_space=pl.ANY)],
        out_specs=vmem,
        scratch_shapes=scratch + [dma((copies,))] * 4,
        compiler_params=pltpu.CompilerParams(
            collective_id=collective_id, has_side_effects=True, vmem_limit_bytes=VMEM_LIMIT
        ),
        name="wide_product",
    )(basis.T, flattened)


def inverse_factor_kernel(gram_ref, o_ref, state):
    size = gram_ref.shape[0]
    row = lax.broadcasted_iota(jnp.int32, (size, size), 0)
    col = lax.broadcasted_iota(jnp.int32, (size, size), 1)
    state[:, :size] = gram_ref[...]
    state[:, size:] = jnp.where(row == col, 1.0, 0.0)
    shape = (8, size)
    place = lax.broadcasted_iota(jnp.int32, shape, 0)
    for start in range(0, size, 8):
        left = state[start : start + 8, :size]
        right = state[start : start + 8, size:]
        columns = [
            jnp.broadcast_to(left[:, start + j : start + j + 1], shape) for j in range(8)
        ]
        scale = jnp.zeros(shape, jnp.float32)
        for j in range(8):

            def pivot_row(value):
                return jnp.broadcast_to(value[j : j + 1], shape)

            inverse = 1.0 / pivot_row(columns[j])
            scale = jnp.where(place == j, inverse, scale)
            if j == 7:
                break
            factor = jnp.where(place > j, columns[j] * inverse, 0.0)
            left = left - factor * pivot_row(left)
            right = right - factor * pivot_row(right)
            for i in range(j + 1, 8):
                columns[i] = columns[i] - factor * pivot_row(columns[i])
        o_ref[start : start + 8, :] = right * jnp.sqrt(scale)
        if start + 8 < size:
            update = jnp.dot(
                (left * scale).T,
                jnp.concatenate([left, right], axis=1),
                precision=lax.Precision.HIGHEST,
                preferred_element_type=jnp.float32,
            )
            state[start + 8 :, :] = state[start + 8 :, :] - update[start + 8 :, :]


def inverse_factor(gram):
    size = gram.shape[0]
    return pl.pallas_call(
        inverse_factor_kernel,
        out_shape=jax.ShapeDtypeStruct(gram.shape, jnp.float32),
        in_specs=[pl.BlockSpec(memory_space=pltpu.VMEM)],
        out_specs=pl.BlockSpec(memory_space=pltpu.VMEM),
        scratch_shapes=[pltpu.VMEM((size, 2 * size), jnp.float32)],
        name="inverse_factor",
    )(gram)


def factor_basis(values, collective_id):
    local_gram = jnp.dot(
        values.T, values, precision=lax.Precision.HIGHEST, preferred_element_type=jnp.float32
    )
    inverse = inverse_factor(summed_gram(local_gram, collective_id))
    return jnp.dot(
        values, inverse.T, precision=lax.Precision.HIGHEST, preferred_element_type=jnp.float32
    )


def on_device(radiance, kernel, test_matrix):
    height, breadth, channels = radiance.shape
    devices = lax.axis_size("gy") * lax.axis_size("gx")
    pixel_count = height * breadth * devices
    smoothed, sketch = smooth_and_sketch(radiance, kernel, test_matrix)
    flattened = smoothed.reshape(height * breadth, channels)
    first_basis = factor_basis(sketch, 0).astype(jnp.bfloat16)
    second = wide_product(first_basis, flattened, 2, True, 1.0)
    basis_out = factor_basis(second, 1) * math.sqrt(pixel_count)
    basis_half = basis_out.astype(jnp.bfloat16)
    scale = math.sqrt(channels) / pixel_count
    coeffs = wide_product(basis_half, flattened, 3, False, scale)
    return (basis_out.reshape(height, breadth, basis_out.shape[1]), coeffs)


def solution(mesh):
    placed = (P("gy", "gx", None), P(), P())
    return jax.shard_map(
        on_device, mesh=mesh, in_specs=placed, out_specs=(P("gy", "gx", None), P()), check_vma=False
    )
```

```python
import functools
import math

import jax
import jax.numpy as jnp
from jax import lax
from jax.experimental import pallas as pl
from jax.experimental.pallas import tpu as pltpu
from jax.sharding import PartitionSpec as P

MESH = pl.DeviceIdType.MESH
LANES = 128
VMEM_LIMIT = 56 * 1024 * 1024


def bit_of(index, bit):
    return (index // 2**bit) % 2


def flipped(index, mask, bits):
    for bit in range(bits):
        if (mask >> bit) & 1:
            index = index + 2**bit * (1 - 2 * bit_of(index, bit))
    return index


def greet(partners):
    barrier = pltpu.get_barrier_semaphore()
    for partner in partners:
        pl.semaphore_signal(barrier, inc=1, device_id=partner, device_id_type=MESH)
    pl.semaphore_wait(barrier, len(partners))


DIRECTIONS = ((1, 0), (-1, 0), (0, 1), (0, -1), (1, 1), (1, -1), (-1, 1), (-1, -1))


def halo_kernel(n_gy, n_gx, x_ref, first_ref, last_ref, c0, c1, c2, c3, *rest):
    outs, (send, recv) = rest[:8], rest[8:]
    height = x_ref.shape[0]
    y, x = lax.axis_index("gy"), lax.axis_index("gx")
    sources = [x_ref.at[height - 1], x_ref.at[0], last_ref, first_ref, c0, c1, c2, c3]
    barrier = pltpu.get_barrier_semaphore()

    def inside(rows, cols):
        return (y + rows >= 0) & (y + rows < n_gy) & (x + cols >= 0) & (x + cols < n_gx)

    present = 0
    for rows, cols in DIRECTIONS:
        there = inside(rows, cols)
        present = present + jnp.where(there, 1, 0)

        @pl.when(there)
        def _():
            pl.semaphore_signal(
                barrier, inc=1, device_id=(y + rows, x + cols), device_id_type=MESH
            )

    pl.semaphore_wait(barrier, present)

    def copy(i):
        rows, cols = DIRECTIONS[i]
        return pltpu.make_async_remote_copy(
            sources[i], outs[i], send.at[i], recv.at[i], (y + rows, x + cols), MESH
        )

    for i, (rows, cols) in enumerate(DIRECTIONS):

        @pl.when(inside(rows, cols))
        def _():
            copy(i).start()

    for i, (rows, cols) in enumerate(DIRECTIONS):
        arrives = inside(-rows, -cols)

        @pl.when(arrives)
        def _():
            copy(i).wait_recv()

        @pl.when(jnp.logical_not(arrives))
        def _():
            outs[i][...] = jnp.zeros_like(outs[i])

    for i, (rows, cols) in enumerate(DIRECTIONS):

        @pl.when(inside(rows, cols))
        def _():
            copy(i).wait_send()


def halos(radiance, collective_id):
    height, width, channels = radiance.shape
    n_gy, n_gx = lax.axis_size("gy"), lax.axis_size("gx")
    first, last = radiance[:, 0], radiance[:, width - 1]
    corners = [
        radiance[row : row + 1, col].astype(jnp.float32)
        for row in (height - 1, 0)
        for col in (width - 1, 0)
    ]
    shapes = [(width, channels)] * 2 + [(height, channels)] * 2 + [(1, channels)] * 4
    kinds = [radiance.dtype] * 4 + [jnp.float32] * 4
    vmem = pl.BlockSpec(memory_space=pltpu.VMEM)
    outs = pl.pallas_call(
        functools.partial(halo_kernel, n_gy, n_gx),
        out_shape=[jax.ShapeDtypeStruct(*each) for each in zip(shapes, kinds)],
        in_specs=[pl.BlockSpec(memory_space=pl.ANY)] + [vmem] * 6,
        out_specs=[vmem] * 8,
        scratch_shapes=[pltpu.SemaphoreType.DMA((8,)), pltpu.SemaphoreType.DMA((8,))],
        compiler_params=pltpu.CompilerParams(collective_id=collective_id, has_side_effects=True),
        name="halo",
    )(radiance, first, last, *corners)
    return outs


def smooth_kernel(
    x_ref, up_ref, down_ref, left_ref, right_ref, c0, c1, c2, c3, k_ref, t_ref, o_ref, s_ref, flat
):
    height, width, block = x_ref.shape
    pitch = width + 8

    @pl.when(pl.program_id(0) == 0)
    def _():
        s_ref[...] = jnp.zeros_like(s_ref)

    for part in range(block // LANES):
        lanes = pl.ds(part * LANES, LANES)

        def fill(h, carry):
            flat[pl.ds(pl.multiple_of((h + 1) * pitch + 8, 8), width), :] = x_ref[h, :, lanes].astype(
                jnp.float32
            )
            return carry

        lax.fori_loop(0, height, fill, 0, unroll=8)
        flat[pl.ds(8, width), :] = up_ref[:, lanes].astype(jnp.float32)
        flat[pl.ds((height + 1) * pitch + 8, width), :] = down_ref[:, lanes].astype(jnp.float32)
        flat[pl.ds(pitch + 7, height, stride=pitch), :] = left_ref[:, lanes].astype(jnp.float32)
        flat[pl.ds(2 * pitch, height, stride=pitch), :] = right_ref[:, lanes].astype(jnp.float32)
        flat[pl.ds(7, 1), :] = c0[:, lanes]
        flat[pl.ds(pitch, 1), :] = c1[:, lanes]
        flat[pl.ds((height + 1) * pitch + 7, 1), :] = c2[:, lanes]
        flat[pl.ds((height + 2) * pitch, 1), :] = c3[:, lanes]
        k = [
            [jnp.broadcast_to(k_ref[a, pl.ds(b, 1), lanes], (16, LANES)) for b in range(3)]
            for a in range(3)
        ]
        for first in range(0, width, 16):

            def shifts(h):
                start = pl.multiple_of(h * pitch, 8) + 7 + first
                return [flat[pl.ds(start + b, 16), :] for b in range(3)]

            def step(h, carry):
                above, here = carry
                below = shifts(h + 2)
                total = [
                    k[0][b] * above[b] + k[1][b] * here[b] + k[2][b] * below[b] for b in range(3)
                ]
                o_ref[h, pl.ds(first, 16), lanes] = (total[0] + total[1] + total[2]).astype(
                    jnp.bfloat16
                )
                return here, below

            lax.fori_loop(0, height, step, (shifts(0), shifts(1)), unroll=8)

    s_ref[...] += jnp.dot(
        o_ref[...].reshape(height * width, block), t_ref[...], preferred_element_type=jnp.float32
    )


def smooth_and_sketch(radiance, kernel, test_matrix):
    height, width, channels = radiance.shape
    k_width = test_matrix.shape[1]
    block = 512
    border = halos(radiance, 4)
    pixels = height * width
    return pl.pallas_call(
        smooth_kernel,
        grid=(channels // block,),
        in_specs=[
            pl.BlockSpec((height, width, block), lambda i: (0, 0, i)),
            pl.BlockSpec((width, block), lambda i: (0, i)),
            pl.BlockSpec((width, block), lambda i: (0, i)),
            pl.BlockSpec((height, block), lambda i: (0, i)),
            pl.BlockSpec((height, block), lambda i: (0, i)),
        ]
        + [pl.BlockSpec((1, block), lambda i: (0, i))] * 4
        + [
            pl.BlockSpec((3, 3, block), lambda i: (0, 0, i)),
            pl.BlockSpec((block, k_width), lambda i: (i, 0)),
        ],
        out_specs=[
            pl.BlockSpec((height, width, block), lambda i: (0, 0, i)),
            pl.BlockSpec((pixels, k_width), lambda i: (0, 0)),
        ],
        out_shape=[
            jax.ShapeDtypeStruct((height, width, channels), jnp.bfloat16),
            jax.ShapeDtypeStruct((pixels, k_width), jnp.float32),
        ],
        scratch_shapes=[
            pltpu.VMEM(((height + 3) * (width + 8), LANES), jnp.float32),
        ],
        compiler_params=pltpu.CompilerParams(vmem_limit_bytes=VMEM_LIMIT),
        cost_estimate=pl.CostEstimate(
            flops=pixels * channels * (2 * k_width + 18),
            bytes_accessed=4 * pixels * channels,
            transcendentals=0,
        ),
        name="smooth_sketch",
    )(radiance, *border, kernel, test_matrix)


def tree_sum(values):
    while len(values) > 1:
        values = [values[i] + values[i + 1] for i in range(0, len(values), 2)]
    return values[0]


def gram_kernel(n_gy, n_gx, x_ref, o_ref, recv_x, recv_y, mine, sx, rx, sy, ry, sg, rg):
    bits_x, bits_y = n_gx.bit_length() - 1, n_gy.bit_length() - 1
    me_x, me_y = lax.axis_index("gx"), lax.axis_index("gy")
    rows = x_ref.shape[0] // n_gx
    along_x = [flipped(me_x, d, bits_x) for d in range(n_gx)]
    along_y = [flipped(me_y, d, bits_y) for d in range(n_gy)]
    greet([(me_y, p) for p in along_x[1:]] + [(p, me_x) for p in along_y[1:]])

    def block(ref, index):
        return ref.at[pl.ds(pl.multiple_of(index * rows, rows), rows), :]

    copies = []
    for d in range(1, n_gx):
        copy = pltpu.make_async_remote_copy(
            block(x_ref, along_x[d]), recv_x.at[d], sx.at[d], rx.at[d], (me_y, along_x[d]), MESH
        )
        copy.start()
        copies.append(copy)
    for copy in copies:
        copy.wait_recv()
    own = x_ref[pl.ds(pl.multiple_of(me_x * rows, rows), rows), :]
    mine[...] = tree_sum([own] + [recv_x[d] for d in range(1, n_gx)])
    later = []
    for d in range(1, n_gy):
        copy = pltpu.make_async_remote_copy(
            mine, recv_y.at[d], sy.at[d], ry.at[d], (along_y[d], me_x), MESH
        )
        copy.start()
        later.append(copy)
    for copy in later:
        copy.wait_recv()
    total = tree_sum([mine[...]] + [recv_y[d] for d in range(1, n_gy)])
    o_ref[pl.ds(pl.multiple_of(me_x * rows, rows), rows), :] = total
    last = []
    for d in range(1, n_gx):
        copy = pltpu.make_async_remote_copy(
            block(o_ref, me_x), block(o_ref, me_x), sg.at[d], rg.at[d], (me_y, along_x[d]), MESH
        )
        copy.start()
        last.append(copy)
    for d in range(1, n_gx):
        pltpu.make_async_remote_copy(
            block(o_ref, along_x[d]), block(o_ref, along_x[d]), sg.at[d], rg.at[d], (me_y, along_x[d]), MESH
        ).wait_recv()
    for copy in copies + later + last:
        copy.wait_send()


def summed_gram(gram, collective_id):
    n_gy, n_gx = lax.axis_size("gy"), lax.axis_size("gx")
    k = gram.shape[0]
    rows = k // n_gx
    dma = pltpu.SemaphoreType.DMA
    return pl.pallas_call(
        functools.partial(gram_kernel, n_gy, n_gx),
        out_shape=jax.ShapeDtypeStruct(gram.shape, jnp.float32),
        in_specs=[pl.BlockSpec(memory_space=pltpu.VMEM)],
        out_specs=pl.BlockSpec(memory_space=pltpu.VMEM),
        scratch_shapes=[
            pltpu.VMEM((n_gx, rows, k), jnp.float32),
            pltpu.VMEM((n_gy, rows, k), jnp.float32),
            pltpu.VMEM((rows, k), jnp.float32),
            dma((n_gx,)),
            dma((n_gx,)),
            dma((n_gy,)),
            dma((n_gy,)),
            dma((n_gx,)),
            dma((n_gx,)),
        ],
        compiler_params=pltpu.CompilerParams(collective_id=collective_id, has_side_effects=True),
        name="gram_sum",
    )(gram)


def wide_orders(n_gy, n_gx, chunks):
    x_steps = [("gx", b, 1) for b in range(n_gx.bit_length() - 1)]
    y_bits = n_gy.bit_length() - 1
    y_steps = [("gy", b, 1) for b in range(max(y_bits - 2, 0))]
    if y_bits >= 2:
        y_steps.append(("gy", y_bits - 2, 2))
    elif y_bits:
        y_steps.append(("gy", 0, 1))
    first, across = x_steps[:1], x_steps[1:]
    return [first + (across[::-1] if q % 2 else across) + y_steps for q in range(chunks)]


def kept_shapes(rows, cols, order):
    shapes = []
    for _, _, bits in order:
        if rows >= 16 * 2**bits:
            rows //= 2**bits
        else:
            cols //= 2**bits
        shapes.append((rows, cols))
    return shapes


def wide_kernel(orders, blocks, again, scale, b_ref, f_ref, *rest):
    o_ref, work, held, load = rest[:4]
    rest = rest[4:]
    gathered = o_ref
    if again:
        gathered, rest = rest[0], rest[1:]
    steps, chunks = len(orders[0]), len(orders)
    recv = [rest[q * steps : (q + 1) * steps] for q in range(chunks)]
    s_send, s_recv, g_send, g_recv = rest[chunks * steps :]
    rows, cols = work.shape
    wide = cols // chunks
    block = cols // blocks
    me = {"gx": lax.axis_index("gx"), "gy": lax.axis_index("gy")}

    def partner(step, d):
        axis, bit, bits = step
        other = dict(me)
        other[axis] = flipped(me[axis], d << bit, bit + bits)
        return (other["gy"], other["gx"])

    loads = [
        pltpu.make_async_copy(f_ref.at[:, pl.ds(i * block, block)], held.at[i], load.at[i])
        for i in range(blocks)
    ]
    for copy in loads:
        copy.start()
    barrier = pltpu.get_barrier_semaphore()
    others = [partner(step, d) for step in orders[0] for d in range(1, 2 ** step[2])]
    for other in others:
        pl.semaphore_signal(barrier, inc=1, device_id=other, device_id_type=MESH)

    places, shapes, index, count = [], [], [], 0
    for q in range(chunks):
        row, col, size = 0, q * wide, (rows, wide)
        shapes.append(kept_shapes(rows, wide, orders[q]))
        places.append([])
        index.append([])
        for s, (axis, bit, bits) in enumerate(orders[q]):
            h, w = shapes[q][s]
            at = []
            for d in range(2**bits):
                part = flipped((me[axis] // 2**bit) % 2**bits, d, bits)
                at.append((row + part * h, col) if h < size[0] else (row, col + part * w))
            places[q].append(at)
            index[q].append(count - 1)
            count += 2**bits - 1
            row, col = at[0]
            size = (h, w)

    def region(q, s, d):
        (row, col), shape = places[q][s][d], shapes[q][s]
        row = row if isinstance(row, int) else pl.multiple_of(row, 16)
        col = col if isinstance(col, int) else pl.multiple_of(col, LANES)
        return (pl.ds(row, shape[0]), pl.ds(col, shape[1]))

    def reduce_copies(q, s):
        copies = []
        for d in range(1, 2 ** orders[q][s][2]):
            sem = index[q][s] + d
            copies.append(
                pltpu.make_async_remote_copy(
                    work.at[region(q, s, d)],
                    recv[q][s].at[d - 1],
                    s_send.at[sem],
                    s_recv.at[sem],
                    partner(orders[q][s], d),
                    MESH,
                )
            )
        return copies

    def gather_copies(q, s, outgoing):
        copies = []
        for d in range(1, 2 ** orders[q][s][2]):
            sem = index[q][s] + d
            at = gathered.at[region(q, s, 0 if outgoing else d)]
            copies.append(
                pltpu.make_async_remote_copy(
                    at, at, g_send.at[sem], g_recv.at[sem], partner(orders[q][s], d), MESH
                )
            )
        return copies

    def start(copies):
        for copy in copies:
            copy.start()

    def advance(q, stage):
        if stage < steps:
            s = stage
            for copy in reduce_copies(q, s):
                copy.wait_recv()
            here = region(q, s, 0)
            parts = [work[here]] + [recv[q][s][d - 1] for d in range(1, 2 ** orders[q][s][2])]
            total = tree_sum(parts)
            if s + 1 < steps:
                work[here] = total
                start(reduce_copies(q, s + 1))
            else:
                gathered[here] = (total * scale).astype(gathered.dtype)
                start(gather_copies(q, s, True))
            return
        s = 2 * steps - 1 - stage
        for copy in gather_copies(q, s, False):
            copy.wait_recv()
        if s > 0:
            start(gather_copies(q, s - 1, True))
        elif again:
            per = wide // block
            for i in range(q * per, (q + 1) * per):
                part = lax.dot_general(
                    held[i],
                    gathered[:, i * block : (i + 1) * block],
                    (((1,), (1,)), ((), ())),
                    preferred_element_type=jnp.float32,
                )
                o_ref[...] = part if i == 0 else o_ref[...] + part

    stages = [0] * chunks
    for q in range(chunks):
        per = wide // block
        for i in range(q * per, (q + 1) * per):
            loads[i].wait()
            work[:, i * block : (i + 1) * block] = jnp.dot(
                b_ref[...], held[i], preferred_element_type=jnp.float32
            )
        if q == 0:
            pl.semaphore_wait(barrier, len(others))
        start(reduce_copies(q, 0))
        if q % 2:
            for p in range(q - 1):
                advance(p, stages[p])
                stages[p] += 1
    while min(stages) < 2 * steps:
        for q in range(chunks):
            if stages[q] < 2 * steps:
                advance(q, stages[q])
                stages[q] += 1
    for q in range(chunks):
        for s in range(steps):
            for copy in reduce_copies(q, s) + gather_copies(q, s, True):
                copy.wait_send()


def wide_product(basis, flattened, collective_id, again, scale):
    n_gy, n_gx = lax.axis_size("gy"), lax.axis_size("gx")
    pixels, cols = flattened.shape
    rows = basis.shape[1]
    chunks = min(8, rows * cols // (16 * LANES * n_gy * n_gx))
    blocks = 8
    orders = wide_orders(n_gy, n_gx, chunks)
    shapes = [kept_shapes(rows, cols // chunks, order) for order in orders]
    copies = chunks * sum(2**bits - 1 for _, _, bits in orders[0])
    dma = pltpu.SemaphoreType.DMA
    scratch = [
        pltpu.VMEM((rows, cols), jnp.float32),
        pltpu.VMEM((blocks, pixels, cols // blocks), jnp.bfloat16),
        dma((blocks,)),
    ]
    if again:
        scratch.append(pltpu.VMEM((rows, cols), jnp.bfloat16))
    for order, of_chunk in zip(orders, shapes):
        for (_, _, bits), shape in zip(order, of_chunk):
            scratch.append(pltpu.VMEM((2**bits - 1, *shape), jnp.float32))
    vmem = pl.BlockSpec(memory_space=pltpu.VMEM)
    return pl.pallas_call(
        functools.partial(wide_kernel, orders, blocks, again, scale),
        out_shape=jax.ShapeDtypeStruct((pixels, rows) if again else (rows, cols), jnp.float32),
        in_specs=[vmem, pl.BlockSpec(memory_space=pl.ANY)],
        out_specs=vmem,
        scratch_shapes=scratch + [dma((copies,))] * 4,
        compiler_params=pltpu.CompilerParams(
            collective_id=collective_id, has_side_effects=True, vmem_limit_bytes=VMEM_LIMIT
        ),
        name="wide_product",
    )(basis.T, flattened)


def inverse_factor_kernel(gram_ref, o_ref, state):
    size = gram_ref.shape[0]
    row = lax.broadcasted_iota(jnp.int32, (size, size), 0)
    col = lax.broadcasted_iota(jnp.int32, (size, size), 1)
    state[:, :size] = gram_ref[...]
    state[:, size:] = jnp.where(row == col, 1.0, 0.0)
    shape = (8, size)
    place = lax.broadcasted_iota(jnp.int32, shape, 0)
    for start in range(0, size, 8):
        left = state[start : start + 8, :size]
        right = state[start : start + 8, size:]
        columns = [
            jnp.broadcast_to(left[:, start + j : start + j + 1], shape) for j in range(8)
        ]
        scale = jnp.zeros(shape, jnp.float32)
        for j in range(8):

            def pivot_row(value):
                return jnp.broadcast_to(value[j : j + 1], shape)

            inverse = 1.0 / pivot_row(columns[j])
            scale = jnp.where(place == j, inverse, scale)
            if j == 7:
                break
            factor = jnp.where(place > j, columns[j] * inverse, 0.0)
            left = left - factor * pivot_row(left)
            right = right - factor * pivot_row(right)
            for i in range(j + 1, 8):
                columns[i] = columns[i] - factor * pivot_row(columns[i])
        o_ref[start : start + 8, :] = right * jnp.sqrt(scale)
        if start + 8 < size:
            update = jnp.dot(
                (left * scale).T,
                jnp.concatenate([left, right], axis=1),
                precision=lax.Precision.HIGHEST,
                preferred_element_type=jnp.float32,
            )
            state[start + 8 :, :] = state[start + 8 :, :] - update[start + 8 :, :]


def inverse_factor(gram):
    size = gram.shape[0]
    return pl.pallas_call(
        inverse_factor_kernel,
        out_shape=jax.ShapeDtypeStruct(gram.shape, jnp.float32),
        in_specs=[pl.BlockSpec(memory_space=pltpu.VMEM)],
        out_specs=pl.BlockSpec(memory_space=pltpu.VMEM),
        scratch_shapes=[pltpu.VMEM((size, 2 * size), jnp.float32)],
        name="inverse_factor",
    )(gram)


def factor_basis(values, collective_id):
    local_gram = jnp.dot(
        values.T, values, precision=lax.Precision.HIGHEST, preferred_element_type=jnp.float32
    )
    inverse = inverse_factor(summed_gram(local_gram, collective_id))
    return jnp.dot(
        values, inverse.T, precision=lax.Precision.HIGHEST, preferred_element_type=jnp.float32
    )


def on_device(radiance, kernel, test_matrix):
    height, breadth, channels = radiance.shape
    devices = lax.axis_size("gy") * lax.axis_size("gx")
    pixel_count = height * breadth * devices
    smoothed, sketch = smooth_and_sketch(radiance, kernel, test_matrix)
    flattened = smoothed.reshape(height * breadth, channels)
    first_basis = factor_basis(sketch, 0).astype(jnp.bfloat16)
    second = wide_product(first_basis, flattened, 2, True, 1.0)
    basis_out = factor_basis(second, 1) * math.sqrt(pixel_count)
    basis_half = basis_out.astype(jnp.bfloat16)
    scale = math.sqrt(channels) / pixel_count
    coeffs = wide_product(basis_half, flattened, 3, False, scale)
    return (basis_out.reshape(height, breadth, basis_out.shape[1]), coeffs)


def solution(mesh):
    placed = (P("gy", "gx", None), P(), P())
    return jax.shard_map(
        on_device, mesh=mesh, in_specs=placed, out_specs=(P("gy", "gx", None), P()), check_vma=False
    )
```
